128 devices in a mesh: path: 16 (over x_hi, y, core), mod: 8 (over x_lo, z).
Axes of the slice: x: 4 (x_hi: 2, x_lo: 2; x = x_hi * 2 + x_lo), y: 4, z: 4, core: 2. Of those that a mesh axis runs over, the one named last changes fastest.
Arguments:
- activations: bfloat16 [16, 512, 4096], P('path', 'mod'), may hold values from -6 to 6
- cotangent: bfloat16 [16, 512, 4096], P('path', 'mod'), may hold values from -6 to 6
- first_weight: bfloat16 [16, 4096, 4096], P('path', None, 'mod'), may hold values from -6 to 6
- second_weight: bfloat16 [16, 4096, 4096], P('path', None, 'mod'), may hold values from -6 to 6
- first_master: float32 [4, 4096, 4096], P(None, ('path', 'mod')), may hold values from -6 to 6
- second_master: float32 [4, 4096, 4096], P(None, ('path', 'mod')), may hold values from -6 to 6
- first_moment: float32 [4, 4096, 4096], P(None, ('path', 'mod')), may hold values from -3 to 3
- second_moment: float32 [4, 4096, 4096], P(None, ('path', 'mod')), may hold values from -3 to 3
- routing: int32 [16, 2], replicated, may hold values from 0 to 3, as said below
Outputs:
- first_result: bfloat16 [16, 4096, 4096], P('path', None, 'mod')
- second_result: bfloat16 [16, 4096, 4096], P('path', None, 'mod')
The draws below stay inside these ranges and needn't reach their ends.
Inputs may be any that keep to these rules, and one draw needn't show every extreme that they name: `routing`: for each of the two levels, every one of the 4 modules is taken by at least one path.
All inputs are finite; a program needn't handle non-finite values.
Results may differ from the reference program's by a relative error of at most 0.0045.
Values may be sent and summed in bfloat16 or wider, within the bound.
No kernel may reach another device: no remote copies, remote signals or barrier semaphores. Data moves between devices by JAX's collectives and lax.ppermute only.
A program may use at most 192 MiB of HBM per device.

```python
import jax
import jax.numpy as jnp
from jax import lax

D = 4096
MODS = 4
TOK = 512
PATHS = 16


def draw_routing(key, part):
    subkeys = jax.random.split(jax.random.fold_in(key, 17), 4)
    columns = []
    for level_index in range(2):
        picked = jax.random.randint(subkeys[level_index], (PATHS,), 0, MODS)
        shuffled = jax.random.permutation(subkeys[level_index + 2], PATHS)
        picked = picked.at[shuffled[:MODS]].set(jnp.arange(MODS))
        columns.append(picked)
    return jnp.stack(columns, axis=1).astype(jnp.int32)


def block_levels(key, dims, pieces, least, high):
    def one(axis_at, parts):
        steps = jax.random.uniform(jax.random.fold_in(jax.random.fold_in(key, 6), axis_at), (parts,), jnp.float32, least / len(pieces), high / len(pieces))
        return jnp.repeat(jnp.exp(steps), dims[axis_at] // parts).reshape((-1,) + (1,) * (len(dims) - axis_at - 1))

    loudness = one(*pieces[0])
    for cut in pieces[1:]:
        loudness = loudness * one(*cut)
    return loudness


def bell_draw(own_key, shape, deviation, most, cuts=(), dtype=jnp.bfloat16):
    level = block_levels(own_key, shape, cuts, -0.22, 0.18) if cuts else 1.0
    entries = jax.random.normal(own_key, shape, jnp.float32) * deviation * level
    return jnp.minimum(jnp.maximum(entries, -most), most).astype(dtype)


def setup_inputs(seed: int = 0) -> dict:
    keys = jax.random.split(jax.random.key(seed), 10)
    return {
        "activations": bell_draw(keys[0], (PATHS, TOK, D), 1.0, 6.0, ((0, 16), (1, 8))),
        "cotangent": bell_draw(keys[1], (PATHS, TOK, D), 1.0, 6.0, ((0, 16), (1, 8))),
        "first_weight": bell_draw(keys[2], (PATHS, D, D), 1.0, 6.0, ((0, 16), (2, 8))),
        "second_weight": bell_draw(keys[3], (PATHS, D, D), 1.0, 6.0, ((0, 16), (2, 8))),
        "first_master": bell_draw(keys[4], (MODS, D, D), 1.0, 6.0, ((1, 128),), jnp.float32),
        "second_master": bell_draw(keys[5], (MODS, D, D), 1.0, 6.0, ((1, 128),), jnp.float32),
        "first_moment": bell_draw(keys[6], (MODS, D, D), 0.5, 3.0, ((1, 128),), jnp.float32),
        "second_moment": bell_draw(keys[7], (MODS, D, D), 0.5, 3.0, ((1, 128),), jnp.float32),
        "routing": draw_routing(jax.random.fold_in(keys[9], 71), 0),
    }


inner_rate = 1.0
outer_rate = 0.7
momentum_decay = 0.9


def path_update(operands):
    inputs_full, upstream, weight_in, weight_out = operands
    scale = D ** -0.5
    pre = jnp.dot(inputs_full, weight_in, preferred_element_type=jnp.float32) * scale
    hidden = jax.nn.silu(pre).astype(jnp.bfloat16)
    grad_hidden = jnp.dot(upstream, weight_out, preferred_element_type=jnp.float32) * scale
    grad_out = lax.dot_general(upstream, hidden, (((0,), (0,)), ((), ())), preferred_element_type=jnp.float32) * scale
    sigma = jax.nn.sigmoid(pre)
    grad_pre = (grad_hidden * sigma * (1.0 + pre * (1.0 - sigma))).astype(jnp.bfloat16)
    grad_in = lax.dot_general(inputs_full, grad_pre, (((0,), (0,)), ((), ())), preferred_element_type=jnp.float32) * scale
    trained_in = (weight_in.astype(jnp.float32) - inner_rate * grad_in).astype(jnp.bfloat16)
    trained_out = (weight_out.astype(jnp.float32) - inner_rate * grad_out).astype(jnp.bfloat16)
    return trained_in, trained_out


def reference(activations, cotangent, first_weight, second_weight, first_master, second_master, first_moment, second_moment, routing):
    trained_in, trained_out = lax.map(path_update, (activations, cotangent, first_weight, second_weight))
    module_ids = jnp.arange(MODS).astype(jnp.int32)
    results = []
    levels = ((trained_in, first_master, first_moment), (trained_out, second_master, second_moment))
    for level_index in range(2):
        trained, master, moment = levels[level_index]
        onehot = (routing[:, level_index][:, None] == module_ids[None, :]).astype(jnp.float32)

        def accumulate(summed, operands):
            weights_row, trained_one = operands
            return summed + weights_row[:, None, None] * trained_one.astype(jnp.float32)[None], None

        summed, _ = lax.scan(accumulate, jnp.zeros(master.shape, jnp.float32), (onehot, trained))
        path_total = jnp.sum(onehot, axis=0)[:, None, None]
        outer = master - summed / path_total
        moment_new = momentum_decay * moment + outer
        renewed = (master - outer_rate * (outer + momentum_decay * moment_new)).astype(jnp.bfloat16)
        results.append(renewed[routing[:, level_index]])
    return results[0], results[1]
```

```python
import functools

import jax
import jax.numpy as jnp
from jax import lax
from jax.experimental import pallas as pl
from jax.experimental.pallas import tpu as pltpu
from jax.sharding import PartitionSpec as P

inner_rate = 1.0
outer_rate = 0.7
momentum_decay = 0.9

ROWS = 256
COLS = 512
HBM = pl.BlockSpec(memory_space=pl.ANY)
SMEM = pl.BlockSpec(memory_space=pltpu.SMEM)
BF = jnp.bfloat16
F32 = jnp.float32


def path_pairs(dxh, dy, dc):
    return [
        ((xh * 4 + y) * 2 + c, ((xh ^ dxh) * 4 + (y + dy) % 4) * 2 + (c ^ dc))
        for xh in range(2)
        for y in range(4)
        for c in range(2)
    ]


def mod_pairs(dxl, dz):
    return [(xl * 4 + z, (xl ^ dxl) * 4 + (z + dz) % 4) for xl in range(2) for z in range(4)]


def over_path(x, dxh, dy, dc):
    return lax.ppermute(x, "path", path_pairs(dxh, dy, dc))


def over_mod(x, dxl, dz):
    return lax.ppermute(x, "mod", mod_pairs(dxl, dz))


def block_of(me, dxh, dy, dc):
    xh, y, c = me // 8, (me // 2) % 4, me % 2
    return (((xh + dxh) % 2) * 4 + (y + dy) % 4) * 2 + (c + dc) % 2


def gather_rows(a):
    half = a.shape[0] // 2
    below = over_mod(a, 0, 1)
    above = over_mod(a, 0, 3)
    side = over_mod(a, 1, 0)
    first = jnp.concatenate([a, below, above, side], axis=0)
    far_a = over_mod(below[:half], 0, 1)
    far_b = over_mod(above[half:], 0, 3)
    side_below = over_mod(side, 0, 1)
    side_above = over_mod(side, 0, 3)
    far = jnp.concatenate([far_a, far_b], axis=0)
    side_far = over_mod(far, 1, 0)
    second = jnp.concatenate([far, side_below, side_above, side_far], axis=0)
    return first, second


def trained_kernel(scale, me_ref, a0, a1, g0, g1, w, out):
    dims = (((0,), (0,)), ((), ()))
    grad = lax.dot_general(a0[...], g0[...], dims, preferred_element_type=F32)
    grad += lax.dot_general(a1[...], g1[...], dims, preferred_element_type=F32)
    out[0] = (w[...].astype(F32) - (inner_rate * scale) * grad).astype(BF)


def trained(me, rows, grads, weight, steps, scale):
    half = rows[0].shape[0]
    dxhs, dys, dcs = zip(*steps)

    def block(i, me_ref):
        def pick(values):
            if len(set(values)) == 1:
                return values[0]
            out = values[0]
            for k, v in enumerate(values[1:], 1):
                out = jnp.where(i == k, v, out)
            return out

        return block_of(me_ref[0], pick(dxhs), pick(dys), pick(dcs))

    n = len(steps)
    return pl.pallas_call(
        functools.partial(trained_kernel, scale),
        out_shape=jax.ShapeDtypeStruct((n, ROWS, COLS), BF),
        grid_spec=pltpu.PrefetchScalarGridSpec(
            num_scalar_prefetch=1,
            grid=(n,),
            in_specs=[
                pl.BlockSpec((half, ROWS), lambda i, m: (0, block(i, m))),
                pl.BlockSpec((half, ROWS), lambda i, m: (0, block(i, m))),
                pl.BlockSpec((half, COLS), lambda i, m: (0, 0)),
                pl.BlockSpec((half, COLS), lambda i, m: (0, 0)),
                pl.BlockSpec((ROWS, COLS), lambda i, m: (block(i, m), 0)),
            ],
            out_specs=pl.BlockSpec((1, ROWS, COLS), lambda i, m: (i, 0, 0)),
        ),
        compiler_params=pltpu.CompilerParams(vmem_limit_bytes=16 << 20),
        cost_estimate=pl.CostEstimate(
            flops=n * 2 * ROWS * COLS * 2 * half,
            bytes_accessed=n * 3 * ROWS * COLS * 2 + 4 * half * COLS,
            transcendentals=0,
        ),
    )(me, *rows, *grads, weight)


def combine(jobs, weights, extra_dtype=BF):
    step = 64
    operands, specs, outs, out_specs, plan = [], [], [], [], []
    for pieces, modules, extra, dtype in jobs:
        first = len(operands)
        for array, block in pieces:
            operands.append(array)
            specs.append(pl.BlockSpec((1, step, COLS), functools.partial(lambda b, i: (b, i, 0), block)))
        if extra is not None:
            operands.append(extra)
            specs.append(pl.BlockSpec((len(modules), step, COLS), lambda i: (0, i, 0)))
        plan.append((first, len(pieces), modules, extra is not None))
        outs.append(jax.ShapeDtypeStruct((len(modules), ROWS, COLS), dtype))
        out_specs.append(pl.BlockSpec((len(modules), step, COLS), lambda i: (0, i, 0)))
    total = len(operands)

    def kernel(w_ref, *refs):
        for j, (first, n, modules, has_extra) in enumerate(plan):
            out = refs[total + j]
            values = [refs[first + k][0].astype(F32) for k in range(n)]
            for o, m in enumerate(modules):
                acc = values[0] * w_ref[0, m]
                for k in range(1, n):
                    acc += values[k] * w_ref[k, m]
                if has_extra:
                    acc += refs[first + n][o].astype(F32)
                out[o] = acc.astype(out.dtype)

    moved = sum(x.size // x.shape[0] * 2 for x in operands)
    return pl.pallas_call(
        kernel,
        out_shape=outs,
        grid=(ROWS // step,),
        in_specs=[SMEM] + specs,
        out_specs=out_specs,
        compiler_params=pltpu.CompilerParams(vmem_limit_bytes=24 << 20),
        cost_estimate=pl.CostEstimate(flops=moved * 4, bytes_accessed=2 * moved, transcendentals=0),
    )(weights, *operands)


def base_kernel(master, moment, out):
    decay = 1.0 + momentum_decay
    a = 1.0 - outer_rate * decay
    b = -outer_rate * momentum_decay * momentum_decay
    out[0] = (a * master[...] + b * moment[...]).astype(out.dtype)


def base_of(master, moment):
    mods, own, width = master.shape
    groups = width // COLS
    spec = pl.BlockSpec((mods, own, COLS), lambda j: (0, 0, j))
    pieces = pl.pallas_call(
        base_kernel,
        out_shape=jax.ShapeDtypeStruct((groups, mods, own, COLS), BF),
        grid=(groups,),
        in_specs=[spec, spec],
        out_specs=pl.BlockSpec((1, mods, own, COLS), lambda j: (j, 0, 0, 0)),
        cost_estimate=pl.CostEstimate(
            flops=3 * master.size, bytes_accessed=10 * master.size, transcendentals=0
        ),
    )(master, moment)
    return lax.all_to_all(pieces, "mod", 0, 0, tiled=True)


def renew(base, keep, halves, whole, factor):
    groups, mods, own, cols = base.shape
    n_half = [len(h) for h in halves]

    def kernel(k_ref, base_ref, keep_ref, *refs):
        outs = refs[-2:]
        low, high = refs[: n_half[0]], refs[n_half[0] : sum(n_half)]
        rest = refs[sum(n_half) : -2]
        for m in range(mods):
            acc = keep_ref[m]
            for h in (low, high)[m // 2]:
                acc += h[m % 2].astype(F32)
            for h in rest:
                acc += h[m].astype(F32)
            outs[m // 2][m % 2] = (base_ref[0, m].astype(F32) + k_ref[m] * acc).astype(BF)

    half_spec = pl.BlockSpec((mods // 2, own, cols), lambda s: (0, s, 0))
    full_spec = pl.BlockSpec((mods, own, cols), lambda s: (0, s, 0))
    shape = jax.ShapeDtypeStruct((mods // 2, groups * own, cols), BF)
    return pl.pallas_call(
        kernel,
        out_shape=(shape, shape),
        grid=(groups,),
        in_specs=[SMEM, pl.BlockSpec((1, mods, own, cols), lambda s: (s, 0, 0, 0)), full_spec]
        + [half_spec] * sum(n_half)
        + [full_spec] * len(whole),
        out_specs=(half_spec, half_spec),
        cost_estimate=pl.CostEstimate(
            flops=6 * keep.size, bytes_accessed=12 * keep.size, transcendentals=0
        ),
    )(factor, base, keep, *halves[0], *halves[1], *whole)


def move(plan, scalars, operands, outs, n_copies, moved, aliases=None):
    n_in = len(operands)

    def kernel(s_ref, *refs):
        ins, targets, sems = refs[:n_in], refs[n_in:-1], refs[-1]
        copies = [
            (cond, pltpu.make_async_copy(src, dst, sems.at[k]))
            for k, (cond, src, dst) in enumerate(plan(s_ref, ins, targets))
        ]
        for act in ("start", "wait"):
            for cond, copy in copies:
                if cond is None:
                    getattr(copy, act)()
                else:
                    pl.when(cond)(getattr(copy, act))

    return pl.pallas_call(
        kernel,
        out_shape=outs,
        in_specs=[SMEM] + [HBM] * n_in,
        out_specs=[HBM] * len(outs),
        scratch_shapes=[pltpu.SemaphoreType.DMA((n_copies,))],
        input_output_aliases=aliases or {},
        cost_estimate=pl.CostEstimate(flops=0, bytes_accessed=2 * moved, transcendentals=0),
    )(scalars, *operands)


def pick(cond_ref, low, high, dst):
    r = cond_ref
    return [
        (r < 2, low.at[jnp.minimum(r, 1)], dst),
        (r >= 2, high.at[jnp.maximum(r - 2, 0)], dst),
    ]


BLOCK = ROWS * COLS * 2
QUARTER = jax.ShapeDtypeStruct((4, ROWS, COLS), BF)
WHOLE = jax.ShapeDtypeStruct((16 * ROWS, COLS), BF)


def body(
    activations,
    cotangent,
    first_weight,
    second_weight,
    first_master,
    second_master,
    first_moment,
    second_moment,
    routing,
):
    weight_in = first_weight[0]
    weight_out = second_weight[0]
    scale = weight_in.shape[0] ** (-0.5)
    me = lax.axis_index("path")
    me_ref = me[None].astype(jnp.int32)
    modules = jnp.arange(first_master.shape[0])

    def route(level, steps):
        return jnp.stack([routing[block_of(me, *s), level] for s in steps])

    def hot(level, steps):
        return (route(level, steps)[:, None] == modules[None, :]).astype(F32)

    acts = gather_rows(activations[0])
    cots = gather_rows(cotangent[0])

    pres = [jnp.dot(a, weight_in, preferred_element_type=F32) * scale for a in acts]
    sigmas = [jax.nn.sigmoid(p) for p in pres]
    hiddens = [(p * s).astype(BF) for p, s in zip(pres, sigmas)]

    order = [(dxh, dy) for dy in range(4) for dxh in range(2)]
    other2 = trained(me_ref, cots, hiddens, weight_out, [(a, b, 1) for a, b in order], scale)
    swapped2 = over_path(other2, 0, 0, 1)
    own2 = trained(me_ref, cots, hiddens, weight_out, [(a, b, 0) for a, b in order], scale)

    grads = []
    for c, p, s in zip(cots, pres, sigmas):
        grad_hidden = jnp.dot(c, weight_out, preferred_element_type=F32) * scale
        grads.append((grad_hidden * s * (1.0 + p * (1.0 - s))).astype(BF))

    def first_rows(dxh, dc):
        return trained(me_ref, acts, grads, weight_in, [(dxh, dy, dc) for dy in range(4)], scale)

    got2 = {}
    for dy in (1, 3, 2):
        block = jnp.concatenate([own2[2 * dy : 2 * dy + 2], swapped2[2 * dy : 2 * dy + 2]], axis=0)
        got2[dy] = over_path(block, 0, dy, 0)
    pieces1 = [
        over_path(first_rows(1, 0), 1, 0, 0),
        over_path(first_rows(1, 1), 1, 0, 1),
        over_path(first_rows(0, 1), 0, 0, 1),
        first_rows(0, 0),
    ]

    base2 = base_of(second_master, second_moment)
    base1 = base_of(first_master, first_moment)

    def factor(level):
        taken = jnp.sum((routing[:, level][:, None] == modules[None, :]).astype(F32), axis=0)
        return (outer_rate * (1.0 + momentum_decay)) / taken

    hot2 = hot(1, [(0, 0, 0), (0, 0, 1), (0, 3, 0), (0, 3, 1), (0, 1, 0), (0, 1, 1), (0, 2, 0), (0, 2, 1)])

    def pieces2(dxh):
        out = [(own2, dxh), (swapped2, dxh)]
        for dy in (1, 3, 2):
            out += [(got2[dy], dxh), (got2[dy], 2 + dxh)]
        return out

    all4 = (0, 1, 2, 3)
    (send2,) = combine([(pieces2(1), all4, None, BF)], hot2)
    arrived2 = over_path(send2, 1, 0, 0)
    (keep2,) = combine([(pieces2(0), all4, None, F32)], hot2)

    hot1 = hot(0, [(1, 0, 0), (1, 0, 1), (0, 0, 1), (0, 0, 0)])

    def at(dy):
        return [(p, dy) for p in pieces1]

    far_low, far_high = combine([(at(2), (0, 1), None, BF), (at(2), (2, 3), None, BF)], hot1)
    part_low = over_path(far_low, 0, 1, 0)
    part_high = over_path(far_high, 0, 3, 0)
    up_high, down_low = combine([(at(1), (2, 3), None, BF), (at(3), (0, 1), None, BF)], hot1)
    up_high = over_path(up_high, 0, 1, 0)
    down_low = over_path(down_low, 0, 3, 0)
    up_low, down_high = combine([(at(1), (0, 1), part_low, BF), (at(3), (2, 3), part_high, BF)], hot1)
    up_low = over_path(up_low, 0, 1, 0)
    down_high = over_path(down_high, 0, 3, 0)
    (keep1,) = combine([(at(0), all4, None, F32)], hot1)

    new2 = renew(base2, keep2, ((), ()), (arrived2,), factor(1))
    new2 = jnp.concatenate(new2, axis=0)
    side2 = over_path(new2, 1, 0, 0)
    around2 = [new2, side2, over_path(new2, 0, 0, 1), over_path(side2, 0, 0, 1)]

    low, high = renew(base1, keep1, ((up_low, down_low), (up_high, down_high)), (), factor(0))
    below = (over_path(low, 0, 1, 0), over_path(high, 0, 1, 0))
    above = (over_path(low, 0, 3, 0), over_path(high, 0, 3, 0))
    far = (over_path(below[0], 0, 1, 0), over_path(above[1], 0, 3, 0))
    rings = [low, high, above[0], above[1], far[0], far[1], below[0], below[1]]

    want2 = jnp.concatenate([route(1, [(0, dy, 0) for dy in range(4)]), me_ref])

    def send_y(dys):
        def plan(s, ins, outs):
            return [
                (None, ins[k].at[s[dy]], outs[j].at[k]) for j, dy in enumerate(dys) for k in range(4)
            ]

        return move(plan, want2, around2, [QUARTER] * len(dys), 4 * len(dys), 4 * len(dys) * BLOCK)

    sent2 = send_y((1, 3, 2))
    came2 = {(-dy) % 4: over_path(x, 0, dy, 0) for dy, x in zip((1, 3, 2), sent2)}

    def rows(out, me, dxh, dy, dc):
        return out.at[pl.ds(pl.multiple_of(block_of(me, dxh, dy, dc) * ROWS, ROWS), ROWS)]

    kinds = [(0, 0), (1, 0), (0, 1), (1, 1)]

    def place2_own(s, ins, outs):
        return [
            (None, ins[k].at[s[0]], rows(outs[0], s[4], dxh, 0, dc)) for k, (dxh, dc) in enumerate(kinds)
        ]

    (result2,) = move(place2_own, want2, around2, [WHOLE], 4, 4 * BLOCK)

    def place2_rest(s, ins, outs):
        return [
            (None, ins[1 + j].at[k], rows(outs[0], s[4], dxh, dy, dc))
            for j, dy in enumerate((3, 1, 2))
            for k, (dxh, dc) in enumerate(kinds)
        ]

    want1 = jnp.concatenate([route(0, [(1, 0, 0), (1, 0, 1), (0, 0, 1), (0, 0, 0)]), me_ref])

    def choose(slots):
        def plan(s, ins, outs):
            out = []
            for j, k in enumerate(slots):
                for dy in range(4):
                    out += pick(s[k], ins[2 * dy], ins[2 * dy + 1], outs[j].at[dy])
            return out

        return move(plan, want1, rings, [QUARTER] * len(slots), 8 * len(slots), 4 * len(slots) * BLOCK)

    to_side, to_cross = choose((0, 1))
    came_side = over_path(to_side, 1, 0, 0)
    came_cross = over_path(to_cross, 1, 0, 1)
    (to_core,) = choose((2,))
    came_core = over_path(to_core, 0, 0, 1)

    def place1_own(s, ins, outs):
        out = []
        for dy in range(4):
            out += pick(s[3], ins[2 * dy], ins[2 * dy + 1], rows(outs[0], s[4], 0, dy, 0))
        return out

    (result1,) = move(place1_own, want1, rings, [WHOLE], 8, 4 * BLOCK)

    def place1_rest(s, ins, outs):
        return [
            (None, ins[1 + j].at[dy], rows(outs[0], s[4], dxh, dy, dc))
            for j, (dxh, dc) in enumerate(((1, 0), (1, 1), (0, 1)))
            for dy in range(4)
        ]

    (result1,) = move(
        place1_rest, want1, [result1, came_side, came_cross, came_core], [WHOLE], 12, 12 * BLOCK, {1: 0}
    )
    (result2,) = move(
        place2_rest, want2, [result2] + [came2[dy] for dy in (3, 1, 2)], [WHOLE], 12, 12 * BLOCK, {1: 0}
    )
    return (result1[None], result2[None])


def solution(mesh):
    return jax.shard_map(
        body,
        mesh=mesh,
        in_specs=(
            P("path", "mod", None),
            P("path", "mod", None),
            P("path", None, "mod"),
            P("path", None, "mod"),
            P(None, ("path", "mod"), None),
            P(None, ("path", "mod"), None),
            P(None, ("path", "mod"), None),
            P(None, ("path", "mod"), None),
            P(),
        ),
        out_specs=(P("path", None, "mod"), P("path", None, "mod")),
        check_vma=False,
    )
```

```python
import functools

import jax
import jax.numpy as jnp
from jax import lax
from jax.experimental import pallas as pl
from jax.experimental.pallas import tpu as pltpu
from jax.sharding import PartitionSpec as P

inner_rate = 1.0
outer_rate = 0.7
momentum_decay = 0.9

ROWS = 256
COLS = 512
HBM = pl.BlockSpec(memory_space=pl.ANY)
BF = jnp.bfloat16
F32 = jnp.float32


def path_pairs(dxh, dy, dc):
    return [
        ((xh * 4 + y) * 2 + c, ((xh ^ dxh) * 4 + (y + dy) % 4) * 2 + (c ^ dc))
        for xh in range(2)
        for y in range(4)
        for c in range(2)
    ]


def mod_pairs(dxl, dz):
    return [(xl * 4 + z, (xl ^ dxl) * 4 + (z + dz) % 4) for xl in range(2) for z in range(4)]


def over_path(x, dxh, dy, dc):
    return lax.ppermute(x, "path", path_pairs(dxh, dy, dc))


def over_mod(x, dxl, dz):
    return lax.ppermute(x, "mod", mod_pairs(dxl, dz))


def block_of(me, dxh, dy, dc):
    xh, y, c = me // 8, (me // 2) % 4, me % 2
    return (((xh + dxh) % 2) * 4 + (y + dy) % 4) * 2 + (c + dc) % 2


def module_of(info, level, step):
    return info[1 + 2 * block_of(info[0], *step) + level]


def call(kernel, info, grid, in_specs, out_specs, outs, operands, flops, aliases=None):
    moved = sum(x.size * x.dtype.itemsize for x in operands)
    return pl.pallas_call(
        kernel,
        out_shape=outs,
        grid_spec=pltpu.PrefetchScalarGridSpec(
            num_scalar_prefetch=1, grid=grid, in_specs=in_specs, out_specs=out_specs
        ),
        input_output_aliases=aliases or {},
        compiler_params=pltpu.CompilerParams(vmem_limit_bytes=24 << 20),
        cost_estimate=pl.CostEstimate(flops=flops, bytes_accessed=moved, transcendentals=0),
    )(info, *operands)


def gather_rows(a):
    half = a.shape[0] // 2
    below = over_mod(a, 0, 1)
    above = over_mod(a, 0, 3)
    side = over_mod(a, 1, 0)
    first = jnp.concatenate([a, below, above, side], axis=0)
    far_a = over_mod(below[:half], 0, 1)
    far_b = over_mod(above[half:], 0, 3)
    side_below = over_mod(side, 0, 1)
    side_above = over_mod(side, 0, 3)
    far = jnp.concatenate([far_a, far_b], axis=0)
    side_far = over_mod(far, 1, 0)
    second = jnp.concatenate([far, side_below, side_above, side_far], axis=0)
    return first, second


def trained_kernel(scale, me_ref, a0, a1, g0, g1, w, out):
    dims = (((0,), (0,)), ((), ()))
    grad = lax.dot_general(a0[...], g0[...], dims, preferred_element_type=F32)
    grad += lax.dot_general(a1[...], g1[...], dims, preferred_element_type=F32)
    out[0] = (w[...].astype(F32) - (inner_rate * scale) * grad).astype(BF)


def trained(me, rows, grads, weight, steps, scale):
    half = rows[0].shape[0]
    dxhs, dys, dcs = zip(*steps)

    def block(i, me_ref):
        def pick(values):
            if len(set(values)) == 1:
                return values[0]
            out = values[0]
            for k, v in enumerate(values[1:], 1):
                out = jnp.where(i == k, v, out)
            return out

        return block_of(me_ref[0], pick(dxhs), pick(dys), pick(dcs))

    n = len(steps)
    return call(
        functools.partial(trained_kernel, scale),
        me,
        (n,),
        [
            pl.BlockSpec((half, ROWS), lambda i, m: (0, block(i, m))),
            pl.BlockSpec((half, ROWS), lambda i, m: (0, block(i, m))),
            pl.BlockSpec((half, COLS), lambda i, m: (0, 0)),
            pl.BlockSpec((half, COLS), lambda i, m: (0, 0)),
            pl.BlockSpec((ROWS, COLS), lambda i, m: (block(i, m), 0)),
        ],
        pl.BlockSpec((1, ROWS, COLS), lambda i, m: (i, 0, 0)),
        jax.ShapeDtypeStruct((n, ROWS, COLS), BF),
        (*rows, *grads, weight),
        n * 4 * ROWS * COLS * half,
    )


def combine(info, level, steps, jobs):
    step = 64
    operands, specs, outs, out_specs, plan = [], [], [], [], []
    for pieces, modules, extra, dtype in jobs:
        first = len(operands)
        for array, block in pieces:
            operands.append(array)
            specs.append(pl.BlockSpec((1, step, COLS), functools.partial(lambda b, i, s: (b, i, 0), block)))
        if extra is not None:
            operands.append(extra)
            specs.append(pl.BlockSpec((len(modules), step, COLS), lambda i, s: (0, i, 0)))
        plan.append((first, len(pieces), modules, extra is not None))
        outs.append(jax.ShapeDtypeStruct((len(modules), ROWS, COLS), dtype))
        out_specs.append(pl.BlockSpec((len(modules), step, COLS), lambda i, s: (0, i, 0)))
    total = len(operands)

    def kernel(info_ref, *refs):
        taken = [module_of(info_ref, level, s) for s in steps]
        for j, (first, n, modules, has_extra) in enumerate(plan):
            out = refs[total + j]
            values = [refs[first + k][0].astype(F32) for k in range(n)]
            for o, m in enumerate(modules):
                acc = None
                for k in range(n):
                    term = values[k] * jnp.where(taken[k] == m, 1.0, 0.0)
                    acc = term if acc is None else acc + term
                if has_extra:
                    acc += refs[first + n][o].astype(F32)
                out[o] = acc.astype(out.dtype)

    flops = 8 * sum(len(p) * len(m) for p, m, _, _ in jobs) * ROWS * COLS
    return call(kernel, info, (ROWS // step,), specs, out_specs, outs, operands, flops)


def base_kernel(master, moment, out):
    decay = 1.0 + momentum_decay
    a = 1.0 - outer_rate * decay
    b = -outer_rate * momentum_decay * momentum_decay
    out[0] = (a * master[...] + b * moment[...]).astype(out.dtype)


def base_of(master, moment):
    mods, own, width = master.shape
    groups = width // COLS
    spec = pl.BlockSpec((mods, own, COLS), lambda j: (0, 0, j))
    return pl.pallas_call(
        base_kernel,
        out_shape=jax.ShapeDtypeStruct((groups, mods, own, COLS), BF),
        grid=(groups,),
        in_specs=[spec, spec],
        out_specs=pl.BlockSpec((1, mods, own, COLS), lambda j: (j, 0, 0, 0)),
        cost_estimate=pl.CostEstimate(
            flops=3 * master.size, bytes_accessed=10 * master.size, transcendentals=0
        ),
    )(master, moment)


def renew(info, level, base, keep, halves, whole, split):
    groups, mods, own, cols = base.shape
    n_half = [len(h) for h in halves]
    n_in = 2 + sum(n_half) + len(whole)
    gain = outer_rate * (1.0 + momentum_decay)

    def kernel(info_ref, base_ref, keep_ref, *refs):
        outs = refs[n_in - 2 :]
        low, high = refs[: n_half[0]], refs[n_half[0] : sum(n_half)]
        rest = refs[sum(n_half) : n_in - 2]
        for m in range(mods):
            taken = 0
            for p in range(16):
                taken += jnp.where(info_ref[1 + 2 * p + level] == m, 1, 0)
            factor = gain / jnp.full((own, cols), taken.astype(F32))
            acc = keep_ref[m]
            for h in (low, high)[m // 2]:
                acc += h[m % 2].astype(F32)
            for h in rest:
                acc += h[m].astype(F32)
            value = (base_ref[0, m].astype(F32) + factor * acc).astype(BF)
            if split:
                outs[m // 2][m % 2] = value
            else:
                outs[0][m] = value

    half_spec = pl.BlockSpec((mods // 2, own, cols), lambda s, i: (0, s, 0))
    full_spec = pl.BlockSpec((mods, own, cols), lambda s, i: (0, s, 0))
    half = jax.ShapeDtypeStruct((mods // 2, groups * own, cols), BF)
    full = jax.ShapeDtypeStruct((mods, groups * own, cols), BF)
    return call(
        kernel,
        info,
        (groups,),
        [pl.BlockSpec((1, mods, own, cols), lambda s, i: (s, 0, 0, 0)), full_spec]
        + [half_spec] * sum(n_half)
        + [full_spec] * len(whole),
        [half_spec, half_spec] if split else [full_spec],
        [half, half] if split else [full],
        (base, keep, *halves[0], *halves[1], *whole),
        8 * keep.size,
    )


def choose(info, level, step, sources):
    rows = 64
    operands, specs = [], []
    for source in sources:
        if len(source) == 1:
            operands += source
            specs.append(
                pl.BlockSpec((1, rows, COLS), lambda i, s: (module_of(s, level, step), i, 0))
            )
        else:
            operands += source
            specs.append(
                pl.BlockSpec(
                    (1, rows, COLS), lambda i, s: (jnp.minimum(module_of(s, level, step), 1), i, 0)
                )
            )
            specs.append(
                pl.BlockSpec(
                    (1, rows, COLS), lambda i, s: (jnp.maximum(module_of(s, level, step) - 2, 0), i, 0)
                )
            )

    def kernel(info_ref, *refs):
        low = module_of(info_ref, level, step) < 2
        out = refs[-1]
        at = 0
        for k, source in enumerate(sources):
            if len(source) == 1:
                out[k] = refs[at][0]
            else:
                @pl.when(low)
                def _(at=at, k=k):
                    out[k] = refs[at][0]

                @pl.when(jnp.logical_not(low))
                def _(at=at, k=k):
                    out[k] = refs[at + 1][0]
            at += len(source)

    n = len(sources)
    return call(
        kernel,
        info,
        (ROWS // rows,),
        specs,
        pl.BlockSpec((n, rows, COLS), lambda i, s: (0, i, 0)),
        jax.ShapeDtypeStruct((n, ROWS, COLS), BF),
        operands,
        n * ROWS * COLS,
    )


def place(info, before, jobs):
    counts = [len(steps) for _, steps in jobs]
    starts = [sum(counts[:j]) for j in range(len(jobs))]
    all_steps = [s for _, steps in jobs for s in steps]

    def out_block(i, s):
        out = block_of(s[0], *all_steps[0])
        for k, step in enumerate(all_steps[1:], 1):
            out = jnp.where(i == k, block_of(s[0], *step), out)
        return (out, 0)

    def in_block(start, count, i, s):
        return (jnp.clip(i - start, 0, count - 1), 0, 0)

    def kernel(info_ref, *refs):
        i = pl.program_id(0)
        for j, (start, count) in enumerate(zip(starts, counts)):
            @pl.when(jnp.logical_and(i >= start, i < start + count))
            def _(j=j):
                refs[-1][...] = refs[j][0]

    specs = [
        pl.BlockSpec((1, ROWS, COLS), functools.partial(in_block, start, count))
        for start, count in zip(starts, counts)
    ]
    operands = [a for a, _ in jobs]
    aliases = {}
    if before is not None:
        operands.append(before)
        specs.append(HBM)
        aliases = {len(operands): 0}
    return call(
        kernel,
        info,
        (len(all_steps),),
        specs,
        pl.BlockSpec((ROWS, COLS), out_block),
        jax.ShapeDtypeStruct((16 * ROWS, COLS), BF),
        operands,
        0,
        aliases,
    )


def body(
    activations,
    cotangent,
    first_weight,
    second_weight,
    first_master,
    second_master,
    first_moment,
    second_moment,
    routing,
):
    weight_in = first_weight[0]
    weight_out = second_weight[0]
    scale = weight_in.shape[0] ** (-0.5)
    info = jnp.concatenate([lax.axis_index("path")[None].astype(jnp.int32), routing.reshape(-1)])

    base1 = base_of(first_master, first_moment)
    base2 = base_of(second_master, second_moment)

    acts = gather_rows(activations[0])
    cots = gather_rows(cotangent[0])

    pres = [jnp.dot(a, weight_in, preferred_element_type=F32) * scale for a in acts]
    sigmas = [jax.nn.sigmoid(p) for p in pres]
    hiddens = [(p * s).astype(BF) for p, s in zip(pres, sigmas)]

    order = [(dxh, dy) for dy in range(4) for dxh in range(2)]
    other2 = trained(info, cots, hiddens, weight_out, [(a, b, 1) for a, b in order], scale)
    swapped2 = over_path(other2, 0, 0, 1)
    own2 = trained(info, cots, hiddens, weight_out, [(a, b, 0) for a, b in order], scale)

    grads = []
    for c, p, s in zip(cots, pres, sigmas):
        grad_hidden = jnp.dot(c, weight_out, preferred_element_type=F32) * scale
        grads.append((grad_hidden * s * (1.0 + p * (1.0 - s))).astype(BF))

    def first_rows(dxh, dc):
        return trained(info, acts, grads, weight_in, [(dxh, dy, dc) for dy in range(4)], scale)

    got2 = {}
    for dy in (1, 3, 2):
        block = jnp.concatenate([own2[2 * dy : 2 * dy + 2], swapped2[2 * dy : 2 * dy + 2]], axis=0)
        got2[dy] = over_path(block, 0, dy, 0)
    pieces1 = [
        over_path(first_rows(1, 0), 1, 0, 0),
        over_path(first_rows(1, 1), 1, 0, 1),
        over_path(first_rows(0, 1), 0, 0, 1),
        first_rows(0, 0),
    ]

    base1 = lax.all_to_all(base1, "mod", 0, 0, tiled=True)
    base2 = lax.all_to_all(base2, "mod", 0, 0, tiled=True)

    steps2 = [(0, dy, dc) for dy in (0, 3, 1, 2) for dc in (0, 1)]

    def pieces2(dxh):
        out = [(own2, dxh), (swapped2, dxh)]
        for dy in (1, 3, 2):
            out += [(got2[dy], dxh), (got2[dy], 2 + dxh)]
        return out

    all4 = (0, 1, 2, 3)
    (send2,) = combine(info, 1, steps2, [(pieces2(1), all4, None, BF)])
    arrived2 = over_path(send2, 1, 0, 0)
    (keep2,) = combine(info, 1, steps2, [(pieces2(0), all4, None, F32)])

    steps1 = [(1, 0, 0), (1, 0, 1), (0, 0, 1), (0, 0, 0)]

    def at(dy):
        return [(p, dy) for p in pieces1]

    def sums(*jobs):
        return combine(info, 0, steps1, jobs)

    far_low, far_high = sums((at(2), (0, 1), None, BF), (at(2), (2, 3), None, BF))
    part_low = over_path(far_low, 0, 1, 0)
    part_high = over_path(far_high, 0, 3, 0)
    up_high, down_low = sums((at(1), (2, 3), None, BF), (at(3), (0, 1), None, BF))
    up_high = over_path(up_high, 0, 1, 0)
    down_low = over_path(down_low, 0, 3, 0)
    up_low, down_high = sums((at(1), (0, 1), part_low, BF), (at(3), (2, 3), part_high, BF))
    up_low = over_path(up_low, 0, 1, 0)
    down_high = over_path(down_high, 0, 3, 0)
    (keep1,) = sums((at(0), all4, None, F32))

    (new2,) = renew(info, 1, base2, keep2, ((), ()), (arrived2,), False)
    side2 = over_path(new2, 1, 0, 0)
    kinds = [(0, 0), (1, 0), (0, 1), (1, 1)]
    around2 = [(new2,), (side2,), (over_path(new2, 0, 0, 1),), (over_path(side2, 0, 0, 1),)]

    low, high = renew(info, 0, base1, keep1, ((up_low, down_low), (up_high, down_high)), (), True)
    below = (over_path(low, 0, 1, 0), over_path(high, 0, 1, 0))
    above = (over_path(low, 0, 3, 0), over_path(high, 0, 3, 0))
    far = (over_path(below[0], 0, 1, 0), over_path(above[1], 0, 3, 0))
    rings = [(low, high), above, far, below]

    came2 = {}
    for dy in (1, 3, 2):
        came2[(-dy) % 4] = over_path(choose(info, 1, (0, dy, 0), around2), 0, dy, 0)
    here2 = choose(info, 1, (0, 0, 0), around2)

    came1 = {}
    for dxh, dc in ((1, 0), (1, 1), (0, 1)):
        came1[dxh, dc] = over_path(choose(info, 0, (dxh, 0, dc), rings), dxh, 0, dc)
    here1 = choose(info, 0, (0, 0, 0), rings)

    def rows1(dxh, dc):
        return [(dxh, dy, dc) for dy in range(4)]

    def rows2(dy):
        return [(dxh, dy, dc) for dxh, dc in kinds]

    result1 = place(info, None, [(here1, rows1(0, 0)), (came1[0, 1], rows1(0, 1))])
    result2 = place(info, None, [(here2, rows2(0))])
    result2 = place(info, result2, [(came2[dy], rows2(dy)) for dy in (3, 1, 2)])
    result1 = place(info, result1, [(came1[1, 0], rows1(1, 0)), (came1[1, 1], rows1(1, 1))])
    return (result1[None], result2[None])


def solution(mesh):
    return jax.shard_map(
        body,
        mesh=mesh,
        in_specs=(
            P("path", "mod", None),
            P("path", "mod", None),
            P("path", None, "mod"),
            P("path", None, "mod"),
            P(None, ("path", "mod"), None),
            P(None, ("path", "mod"), None),
            P(None, ("path", "mod"), None),
            P(None, ("path", "mod"), None),
            P(),
        ),
        out_specs=(P("path", None, "mod"), P("path", None, "mod")),
        check_vma=False,
    )
```

```python
import functools

import jax
import jax.numpy as jnp
from jax import lax
from jax.experimental import pallas as pl
from jax.experimental.pallas import tpu as pltpu
from jax.sharding import PartitionSpec as P

inner_rate = 1.0
outer_rate = 0.7
momentum_decay = 0.9

ROWS = 256
COLS = 512
HBM = pl.BlockSpec(memory_space=pl.ANY)
VMEM = pl.BlockSpec(memory_space=pltpu.VMEM)
SMEM = pl.BlockSpec(memory_space=pltpu.SMEM)
BF = jnp.bfloat16
F32 = jnp.float32


def path_pairs(dxh, dy, dc):
    return [
        ((xh * 4 + y) * 2 + c, ((xh ^ dxh) * 4 + (y + dy) % 4) * 2 + (c ^ dc))
        for xh in range(2)
        for y in range(4)
        for c in range(2)
    ]


def mod_pairs(dxl, dz):
    return [(xl * 4 + z, (xl ^ dxl) * 4 + (z + dz) % 4) for xl in range(2) for z in range(4)]


def over_path(x, dxh, dy, dc):
    return lax.ppermute(x, "path", path_pairs(dxh, dy, dc))


def over_mod(x, dxl, dz):
    return lax.ppermute(x, "mod", mod_pairs(dxl, dz))


def block_of(me, dxh, dy, dc):
    xh, y, c = me // 8, (me // 2) % 4, me % 2
    return (((xh + dxh) % 2) * 4 + (y + dy) % 4) * 2 + (c + dc) % 2


def module_of(info, level, step):
    return info[1 + 2 * block_of(info[0], *step) + level]


def call(kernel, info, grid, in_specs, out_specs, outs, operands, flops, aliases=None):
    moved = sum(x.size * x.dtype.itemsize for x in operands)
    return pl.pallas_call(
        kernel,
        out_shape=outs,
        grid_spec=pltpu.PrefetchScalarGridSpec(
            num_scalar_prefetch=1, grid=grid, in_specs=in_specs, out_specs=out_specs
        ),
        input_output_aliases=aliases or {},
        compiler_params=pltpu.CompilerParams(vmem_limit_bytes=24 << 20),
        cost_estimate=pl.CostEstimate(flops=1, bytes_accessed=1, transcendentals=0),
    )(info, *operands)


def whole(kernel, info, operands, outs, flops, earlier=()):
    n_in, n_wait = len(operands), len(earlier)

    def run(info_ref, *refs):
        kernel(info_ref, refs[:n_in], refs[n_in + n_wait :])

    moved = sum(x.size * x.dtype.itemsize for x in operands)
    return pl.pallas_call(
        run,
        out_shape=outs,
        in_specs=[SMEM] + [VMEM] * (n_in + n_wait),
        out_specs=[VMEM] * len(outs),
        compiler_params=pltpu.CompilerParams(vmem_limit_bytes=8 << 20),
        cost_estimate=pl.CostEstimate(flops=1, bytes_accessed=1, transcendentals=0),
    )(info, *operands, *earlier)


def block(*lead, dtype=BF):
    return jax.ShapeDtypeStruct((*lead, ROWS, COLS), dtype)


def lay(info, arrays, earlier=()):
    flat = [x for a in arrays for x in (a if isinstance(a, tuple) else (a,))]
    kinds = [isinstance(a, tuple) for a in arrays]
    rows, width = (arrays[0][0].shape if kinds[0] else arrays[0].shape[1:])

    def kernel(info_ref, ins, outs):
        at = 0
        for k, pair in enumerate(kinds):
            for j in range(2):
                x = ins[at + j][...] if pair else ins[at][j]
                outs[j][k * rows : (k + 1) * rows, :] = x
            at += 2 if pair else 1

    out = jax.ShapeDtypeStruct((rows * len(arrays), width), BF)
    return whole(kernel, info, flat, [out, out], 0, earlier)


def gather_rows(info, a, c):
    def stack(info_ref, ins, outs):
        outs[0][0] = ins[0][...]
        outs[0][1] = ins[1][...]

    (both,) = whole(stack, info, (a, c), [jax.ShapeDtypeStruct((2, *a.shape), BF)], 0)
    below, above, side = over_mod(both, 0, 1), over_mod(both, 0, 3), over_mod(both, 1, 0)
    far = (over_mod(below[0], 0, 1), over_mod(above[1], 0, 3))
    side_below, side_above = over_mod(side, 0, 1), over_mod(side, 0, 3)
    side_far = tuple(over_mod(x, 1, 0) for x in far)
    first = lay(info, [both, below, above, side], far)
    second = lay(info, [far, side_below, side_above, side_far])
    return tuple(zip(first, second))


def trained(info, rows, grads, weight, groups, scale, earlier=()):
    def kernel(info_ref, ins, outs):
        a0, a1, g0, g1, w = ins
        dims = (((0,), (0,)), ((), ()))
        for out, steps in zip(outs, groups):
            for k, step in enumerate(steps):
                start = pl.multiple_of(block_of(info_ref[0], *step) * ROWS, ROWS)
                at = pl.ds(start, ROWS)
                grad = lax.dot_general(a0[:, at], g0[...], dims, preferred_element_type=F32)
                grad += lax.dot_general(a1[:, at], g1[...], dims, preferred_element_type=F32)
                out[k] = (w[at, :].astype(F32) - (inner_rate * scale) * grad).astype(BF)

    n = sum(len(g) for g in groups)
    return whole(
        kernel,
        info,
        (*rows, *grads, weight),
        [block(len(g)) for g in groups],
        n * 4 * ROWS * COLS * rows[0].shape[0],
        earlier,
    )


def join(info, arrays, first, earlier=()):
    n, rows = arrays[0].shape[0] - first, ROWS // 2
    assert n == first

    def kernel(info_ref, *refs):
        for k in range(len(arrays)):
            refs[-1][k * n : (k + 1) * n] = refs[k][...]

    return call(
        kernel,
        info,
        (ROWS // rows,),
        [pl.BlockSpec((n, rows, COLS), lambda i, s: (1, i, 0))] * len(arrays) + [HBM] * len(earlier),
        pl.BlockSpec((n * len(arrays), rows, COLS), lambda i, s: (0, i, 0)),
        block(n * len(arrays)),
        (*arrays, *earlier),
        0,
    )


def combine(info, level, steps, jobs, earlier=()):
    rows, step = ROWS // 2, 16
    operands, specs, outs, out_specs, plan = [], [], [], [], []
    for pieces, modules, extra, dtype in jobs:
        first = len(operands)
        for array, at in pieces:
            operands.append(array)
            specs.append(pl.BlockSpec((1, rows, COLS), functools.partial(lambda b, i, s: (b, i, 0), at)))
        both = pl.BlockSpec((len(modules), rows, COLS), lambda i, s: (0, i, 0))
        if extra is not None:
            operands.append(extra)
            specs.append(both)
        plan.append((first, len(pieces), modules, extra is not None))
        outs.append(block(len(modules), dtype=dtype))
        out_specs.append(both)
    n_in = len(operands) + len(earlier)

    def kernel(info_ref, *refs):
        taken = [module_of(info_ref, level, s) for s in steps]
        gate = [[jnp.where(t == m, 1.0, 0.0) for m in range(4)] for t in taken]

        @pl.loop(0, rows // step)
        def _(i):
            at = pl.ds(pl.multiple_of(i * step, step), step)
            for (first, n, modules, has_extra), out in zip(plan, refs[n_in:]):
                values = [refs[first + k][0, at, :].astype(F32) for k in range(n)]
                for o, m in enumerate(modules):
                    acc = values[0] * gate[0][m]
                    for k in range(1, n):
                        acc += values[k] * gate[k][m]
                    if has_extra:
                        acc += refs[first + n][o, at, :].astype(F32)
                    out[o, at, :] = acc.astype(out.dtype)

    specs += [HBM] * len(earlier)
    return call(kernel, info, (ROWS // rows,), specs, out_specs, outs, (*operands, *earlier), 0)


def base_of(info, masters, moments, earlier=()):
    mods, own, width = masters[0].shape
    decay = 1.0 + momentum_decay
    a = 1.0 - outer_rate * decay
    b = -outer_rate * momentum_decay * momentum_decay

    def kernel(info_ref, m1, m2, v1, v2, *refs):
        for level, (m, v) in enumerate(((m1, v1), (m2, v2))):
            refs[-1][0, level * mods : (level + 1) * mods] = (a * m[...] + b * v[...]).astype(BF)

    spec = pl.BlockSpec((mods, own, COLS), lambda j, s: (0, 0, j))
    return call(
        kernel,
        info,
        (width // COLS,),
        [spec] * 4 + [HBM] * len(earlier),
        pl.BlockSpec((1, 2 * mods, own, COLS), lambda j, s: (j, 0, 0, 0)),
        jax.ShapeDtypeStruct((width // COLS, 2 * mods, own, COLS), BF),
        (*masters, *moments, *earlier),
        6 * masters[0].size,
    )


def renew(factor, base, first, keep, halves, wholes, split, earlier=()):
    groups, _, own, cols = base.shape
    mods = keep.shape[0]
    n_half = [len(h) for h in halves]
    n_in = 2 + sum(n_half) + len(wholes) + len(earlier)

    def kernel(factor_ref, base_ref, keep_ref, *refs):
        outs = refs[n_in - 2 :]
        low, high = refs[: n_half[0]], refs[n_half[0] : sum(n_half)]
        rest = refs[sum(n_half) : sum(n_half) + len(wholes)]
        for s in range(2):
            at = slice(s * own, (s + 1) * own)
            for m in range(mods):
                acc = keep_ref[m, at, :]
                for h in (low, high)[m // 2]:
                    acc += h[m % 2, at, :].astype(F32)
                for h in rest:
                    acc += h[m, at, :].astype(F32)
                value = (base_ref[s, m].astype(F32) + factor_ref[m] * acc).astype(BF)
                if split:
                    outs[m // 2][m % 2, at, :] = value
                else:
                    outs[0][m, at, :] = value

    half_spec = pl.BlockSpec((mods // 2, 2 * own, cols), lambda s, i: (0, s, 0))
    full_spec = pl.BlockSpec((mods, 2 * own, cols), lambda s, i: (0, s, 0))
    return call(
        kernel,
        factor,
        (groups // 2,),
        [pl.BlockSpec((2, mods, own, cols), lambda s, i: (s, first // mods, 0, 0)), full_spec]
        + [half_spec] * sum(n_half)
        + [full_spec] * len(wholes)
        + [HBM] * len(earlier),
        [half_spec] * 2 if split else [full_spec],
        [block(mods // 2)] * 2 if split else [block(mods)],
        (base, keep, *halves[0], *halves[1], *wholes, *earlier),
        0,
    )


def choose(info, level, steps, sources):
    rows = ROWS // 2
    operands, specs = [], []

    def spec(index):
        return pl.BlockSpec((1, rows, COLS), lambda i, s: (index(s), i, 0))

    for step in steps:
        for source in sources:
            operands += source
            if len(source) == 1:
                specs.append(spec(lambda s, t=step: module_of(s, level, t)))
            else:
                specs.append(spec(lambda s, t=step: jnp.minimum(module_of(s, level, t), 1)))
                specs.append(spec(lambda s, t=step: jnp.maximum(module_of(s, level, t) - 2, 0)))
    n = len(sources)

    def kernel(info_ref, *refs):
        at = 0
        for j, step in enumerate(steps):
            low = module_of(info_ref, level, step) < 2
            out = refs[len(operands) + j]
            for k, source in enumerate(sources):
                if len(source) == 1:
                    out[k] = refs[at][0]
                else:
                    @pl.when(low)
                    def _(at=at, k=k, out=out):
                        out[k] = refs[at][0]

                    @pl.when(jnp.logical_not(low))
                    def _(at=at, k=k, out=out):
                        out[k] = refs[at + 1][0]
                at += len(source)

    return call(
        kernel,
        info,
        (ROWS // rows,),
        specs,
        [pl.BlockSpec((n, rows, COLS), lambda i, s: (0, i, 0))] * len(steps),
        [block(n)] * len(steps),
        operands,
        0,
    )


def place(info, befores, jobs, earlier=()):
    n_in, n = len(jobs), sum(len(steps) for _, steps, _ in jobs)
    results = 1 + max(r for _, _, r in jobs)
    rest = list(befores) + list(earlier)

    def kernel(info_ref, *refs):
        sems = refs[-1]
        outs = refs[-1 - results : -1]
        copies = []
        for j, (_, steps, r) in enumerate(jobs):
            for k, step in enumerate(steps):
                start = pl.multiple_of(block_of(info_ref[0], *step) * ROWS, ROWS)
                target = outs[r].at[pl.ds(start, ROWS)]
                copies.append(pltpu.make_async_copy(refs[j].at[k], target, sems.at[len(copies)]))
        for copy in copies:
            copy.start()
        for copy in copies:
            copy.wait()

    return pl.pallas_call(
        kernel,
        out_shape=[jax.ShapeDtypeStruct((16 * ROWS, COLS), BF)] * results,
        in_specs=[SMEM] + [VMEM] * n_in + [HBM] * len(rest),
        out_specs=[HBM] * results,
        scratch_shapes=[pltpu.SemaphoreType.DMA((n,))],
        input_output_aliases={1 + n_in + k: k for k in range(len(befores))},
        compiler_params=pltpu.CompilerParams(vmem_limit_bytes=24 << 20),
        cost_estimate=pl.CostEstimate(flops=1, bytes_accessed=1, transcendentals=0),
    )(info, *[a for a, _, _ in jobs], *rest)


def body(
    activations,
    cotangent,
    first_weight,
    second_weight,
    first_master,
    second_master,
    first_moment,
    second_moment,
    routing,
):
    weight_in = first_weight[0]
    weight_out = second_weight[0]
    scale = weight_in.shape[0] ** (-0.5)
    info = jnp.concatenate([lax.axis_index("path")[None].astype(jnp.int32), routing.reshape(-1)])

    def factor_of(level):
        taken = jnp.sum((routing[:, level][:, None] == jnp.arange(4)[None, :]).astype(F32), axis=0)
        return (outer_rate * (1.0 + momentum_decay)) / taken

    factor1, factor2 = factor_of(0), factor_of(1)

    masters, moments = (first_master, second_master), (first_moment, second_moment)
    acts, cots = gather_rows(info, activations[0], cotangent[0])

    pres = [jnp.dot(a, weight_in, preferred_element_type=F32) * scale for a in acts]
    sigmas = [jax.nn.sigmoid(p) for p in pres]
    hiddens = [(p * s).astype(BF) for p, s in zip(pres, sigmas)]
    grads = []
    for c, p, s in zip(cots, pres, sigmas):
        grad_hidden = jnp.dot(c, weight_out, preferred_element_type=F32) * scale
        grads.append((grad_hidden * s * (1.0 + p * (1.0 - s))).astype(BF))

    def first_rows(kinds, *earlier):
        groups = [[(dxh, dy, dc) for dy in range(4)] for dxh, dc in kinds]
        return trained(info, acts, grads, weight_in, groups, scale, earlier)

    (to_core,) = first_rows([(0, 1)])
    from_core = over_path(to_core, 0, 0, 1)

    here2, up2, far2, down2 = trained(
        info, cots, hiddens, weight_out,
        [[(dxh, dy, dc) for dc in range(2) for dxh in range(2)] for dy in range(4)], scale,
        (to_core,),
    )
    got2 = [here2, over_path(far2, 0, 2, 0), over_path(up2, 0, 1, 0), over_path(down2, 0, 3, 0)]
    to_side, to_cross, here1 = first_rows([(1, 0), (1, 1), (0, 0)], from_core, here2)
    pieces1 = [over_path(to_side, 1, 0, 0), over_path(to_cross, 1, 0, 1), from_core, here1]

    base = base_of(info, masters, moments, (here1,))

    all4 = (0, 1, 2, 3)
    steps1 = [(1, 0, 0), (1, 0, 1), (0, 0, 1), (0, 0, 0)]

    def at(dy):
        return [(p, dy) for p in pieces1]

    def sums(*jobs, earlier=()):
        return combine(info, 0, steps1, jobs, earlier)

    far_low, far_high, up_high, down_low = sums(
        (at(2), (0, 1), None, BF),
        (at(2), (2, 3), None, BF),
        (at(1), (2, 3), None, BF),
        (at(3), (0, 1), None, BF),
        earlier=(base,),
    )
    part_low = over_path(far_low, 0, 1, 0)
    part_high = over_path(far_high, 0, 3, 0)
    up_high = over_path(up_high, 0, 1, 0)
    down_low = over_path(down_low, 0, 3, 0)

    for_core2 = join(info, got2, 2, (far_low,))
    base = lax.all_to_all(base, "mod", 0, 0, tiled=True)
    swapped2 = over_path(for_core2, 0, 0, 1)
    steps2 = [(0, dy, dc) for dc in (0, 1) for dy in (0, 2, 3, 1)]

    def pieces2(dxh):
        return [(x, dxh) for x in got2] + [(swapped2, 2 * k + dxh) for k in range(4)]

    (send2,) = combine(info, 1, steps2, [(pieces2(1), all4, None, BF)])
    arrived2 = over_path(send2, 1, 0, 0)

    up_low, down_high = sums(
        (at(1), (0, 1), part_low, BF), (at(3), (2, 3), part_high, BF), earlier=(send2,)
    )
    up_low = over_path(up_low, 0, 1, 0)
    down_high = over_path(down_high, 0, 3, 0)
    (keep1,) = sums((at(0), all4, None, F32))
    (keep2,) = combine(info, 1, steps2, [(pieces2(0), all4, None, F32)], (keep1,))

    low, high = renew(factor1, base, 0, keep1, ((up_low, down_low), (up_high, down_high)), (), True)
    below = (over_path(low, 0, 1, 0), over_path(high, 0, 1, 0))
    above = (over_path(low, 0, 3, 0), over_path(high, 0, 3, 0))
    far = (over_path(below[0], 0, 1, 0), over_path(above[1], 0, 3, 0))
    rings = [(low, high), above, far, below]

    (new2,) = renew(factor2, base, 4, keep2, ((), ()), (arrived2,), False, (low,))
    side2 = over_path(new2, 1, 0, 0)
    kinds = [(0, 0), (1, 0), (0, 1), (1, 1)]
    around2 = [(new2,), (side2,), (over_path(new2, 0, 0, 1),), (over_path(side2, 0, 0, 1),)]

    def rows1(dxh, dc):
        return [(dxh, dy, dc) for dy in range(4)]

    def rows2(dy):
        return [(dxh, dy, dc) for dxh, dc in kinds]

    to_far, to_up, to_down = choose(info, 1, [(0, dy, 0) for dy in (2, 1, 3)], around2)
    came2 = {2: over_path(to_far, 0, 2, 0), 3: over_path(to_up, 0, 1, 0), 1: over_path(to_down, 0, 3, 0)}
    (here2,) = choose(info, 1, [(0, 0, 0)], around2)
    to_side, to_cross = choose(info, 0, [(1, 0, 0), (1, 0, 1)], rings)
    to_core, here1 = choose(info, 0, [(0, 0, 1), (0, 0, 0)], rings)
    came1 = {
        (1, 0): over_path(to_side, 1, 0, 0),
        (1, 1): over_path(to_cross, 1, 0, 1),
        (0, 1): over_path(to_core, 0, 0, 1),
    }

    results = place(
        info,
        (),
        [(here1, rows1(0, 0), 0), (came1[0, 1], rows1(0, 1), 0), (here2, rows2(0), 1)],
    )
    results = place(
        info,
        results,
        [(came1[1, 0], rows1(1, 0), 0), (came1[1, 1], rows1(1, 1), 0)]
        + [(came2[dy], rows2(dy), 1) for dy in (2, 3, 1)],
    )
    return (results[0][None], results[1][None])


def solution(mesh):
    return jax.shard_map(
        body,
        mesh=mesh,
        in_specs=(
            P("path", "mod", None),
            P("path", "mod", None),
            P("path", None, "mod"),
            P("path", None, "mod"),
            P(None, ("path", "mod"), None),
            P(None, ("path", "mod"), None),
            P(None, ("path", "mod"), None),
            P(None, ("path", "mod"), None),
            P(),
        ),
        out_specs=(P("path", None, "mod"), P("path", None, "mod")),
        check_vma=False,
    )
```

```python
import functools

import jax
import jax.numpy as jnp
from jax import lax
from jax.experimental import pallas as pl
from jax.experimental.pallas import tpu as pltpu
from jax.sharding import PartitionSpec as P

inner_rate = 1.0
outer_rate = 0.7
momentum_decay = 0.9

ROWS = 256
COLS = 512
HBM = pl.BlockSpec(memory_space=pl.ANY)
VMEM = pl.BlockSpec(memory_space=pltpu.VMEM)
SMEM = pl.BlockSpec(memory_space=pltpu.SMEM)
BF = jnp.bfloat16
F32 = jnp.float32


def path_pairs(dxh, dy, dc):
    return [
        ((xh * 4 + y) * 2 + c, ((xh ^ dxh) * 4 + (y + dy) % 4) * 2 + (c ^ dc))
        for xh in range(2)
        for y in range(4)
        for c in range(2)
    ]


def mod_pairs(dxl, dz):
    return [(xl * 4 + z, (xl ^ dxl) * 4 + (z + dz) % 4) for xl in range(2) for z in range(4)]


def over_path(x, dxh, dy, dc):
    return lax.ppermute(x, "path", path_pairs(dxh, dy, dc))


def over_mod(x, dxl, dz):
    return lax.ppermute(x, "mod", mod_pairs(dxl, dz))


def block_of(me, dxh, dy, dc):
    xh, y, c = me // 8, (me // 2) % 4, me % 2
    return (((xh + dxh) % 2) * 4 + (y + dy) % 4) * 2 + (c + dc) % 2


def module_of(info, level, step):
    return info[1 + 2 * block_of(info[0], *step) + level]


def call(kernel, info, grid, in_specs, out_specs, outs, operands, flops, aliases=None):
    moved = sum(x.size * x.dtype.itemsize for x in operands)
    return pl.pallas_call(
        kernel,
        out_shape=outs,
        grid_spec=pltpu.PrefetchScalarGridSpec(
            num_scalar_prefetch=1, grid=grid, in_specs=in_specs, out_specs=out_specs
        ),
        input_output_aliases=aliases or {},
        compiler_params=pltpu.CompilerParams(vmem_limit_bytes=24 << 20),
        cost_estimate=pl.CostEstimate(flops=1, bytes_accessed=1, transcendentals=0),
    )(info, *operands)


def whole(kernel, info, operands, outs, flops, earlier=()):
    n_in, n_wait = len(operands), len(earlier)

    def run(info_ref, *refs):
        kernel(info_ref, refs[:n_in], refs[n_in + n_wait :])

    moved = sum(x.size * x.dtype.itemsize for x in operands)
    return pl.pallas_call(
        run,
        out_shape=outs,
        in_specs=[SMEM] + [VMEM] * (n_in + n_wait),
        out_specs=[VMEM] * len(outs),
        compiler_params=pltpu.CompilerParams(vmem_limit_bytes=8 << 20),
        cost_estimate=pl.CostEstimate(flops=1, bytes_accessed=1, transcendentals=0),
    )(info, *operands, *earlier)


def block(*lead, dtype=BF):
    return jax.ShapeDtypeStruct((*lead, ROWS, COLS), dtype)


def lay(info, arrays, earlier=()):
    flat = [x for a in arrays for x in (a if isinstance(a, tuple) else (a,))]
    kinds = [isinstance(a, tuple) for a in arrays]
    rows, width = (arrays[0][0].shape if kinds[0] else arrays[0].shape[1:])

    def kernel(info_ref, ins, outs):
        at = 0
        for k, pair in enumerate(kinds):
            for j in range(2):
                x = ins[at + j][...] if pair else ins[at][j]
                outs[j][k * rows : (k + 1) * rows, :] = x
            at += 2 if pair else 1

    out = jax.ShapeDtypeStruct((rows * len(arrays), width), BF)
    return whole(kernel, info, flat, [out, out], 0, earlier)


def gather_rows(info, a, c):
    def stack(a_ref, c_ref, out, sems):
        copies = [
            pltpu.make_async_copy(x, out.at[k], sems.at[k]) for k, x in enumerate((a_ref, c_ref))
        ]
        for copy in copies:
            copy.start()
        for copy in copies:
            copy.wait()

    both = pl.pallas_call(
        stack,
        out_shape=jax.ShapeDtypeStruct((2, *a.shape), BF),
        in_specs=[pl.BlockSpec(memory_space=pltpu.HBM)] * 2,
        out_specs=VMEM,
        scratch_shapes=[pltpu.SemaphoreType.DMA((2,))],
        cost_estimate=pl.CostEstimate(flops=1, bytes_accessed=1, transcendentals=0),
    )(a, c)
    below, above, side = over_mod(both, 0, 1), over_mod(both, 0, 3), over_mod(both, 1, 0)
    far = (over_mod(below[0], 0, 1), over_mod(above[1], 0, 3))
    side_below, side_above = over_mod(side, 0, 1), over_mod(side, 0, 3)
    side_far = tuple(over_mod(x, 1, 0) for x in far)
    first = lay(info, [both, below, above, side], far)
    second = lay(info, [far, side_below, side_above, side_far])
    return tuple(zip(first, second))


def trained(info, rows, grads, weight, groups, scale, earlier=()):
    def kernel(info_ref, ins, outs):
        a0, a1, g0, g1, w = ins
        dims = (((0,), (0,)), ((), ()))
        for out, steps in zip(outs, groups):
            for k, step in enumerate(steps):
                start = pl.multiple_of(block_of(info_ref[0], *step) * ROWS, ROWS)
                at = pl.ds(start, ROWS)
                grad = lax.dot_general(a0[:, at], g0[...], dims, preferred_element_type=F32)
                grad += lax.dot_general(a1[:, at], g1[...], dims, preferred_element_type=F32)
                out[k] = (w[at, :].astype(F32) - (inner_rate * scale) * grad).astype(BF)

    n = sum(len(g) for g in groups)
    return whole(
        kernel,
        info,
        (*rows, *grads, weight),
        [block(len(g)) for g in groups],
        n * 4 * ROWS * COLS * rows[0].shape[0],
        earlier,
    )


def join(info, arrays, earlier=()):
    n, rows = arrays[0].shape[0] // 2, ROWS // 2

    def kernel(info_ref, *refs):
        for k in range(len(arrays)):
            refs[-2][k * n : (k + 1) * n] = refs[k][:n]
            refs[-1][k * n : (k + 1) * n] = refs[k][n:]

    out = pl.BlockSpec((n * len(arrays), rows, COLS), lambda i, s: (0, i, 0))
    return call(
        kernel,
        info,
        (ROWS // rows,),
        [pl.BlockSpec((2 * n, rows, COLS), lambda i, s: (0, i, 0))] * len(arrays) + [HBM] * len(earlier),
        [out, out],
        [block(n * len(arrays))] * 2,
        (*arrays, *earlier),
        0,
    )


def combine(info, level, steps, jobs, earlier=()):
    rows, step = ROWS // 2, 16
    operands, specs, outs, out_specs, plan = [], [], [], [], []
    for pieces, modules, extra, dtype in jobs:
        first = len(operands)
        for array, at in pieces:
            operands.append(array)
            specs.append(pl.BlockSpec((1, rows, COLS), functools.partial(lambda b, i, s: (b, i, 0), at)))
        both = pl.BlockSpec((len(modules), rows, COLS), lambda i, s: (0, i, 0))
        if extra is not None:
            operands.append(extra)
            specs.append(both)
        plan.append((first, len(pieces), modules, extra is not None))
        outs.append(block(len(modules), dtype=dtype))
        out_specs.append(both)
    n_in = len(operands) + len(earlier)

    def kernel(info_ref, *refs):
        taken = [module_of(info_ref, level, s) for s in steps]
        gate = [[jnp.where(t == m, 1.0, 0.0) for m in range(4)] for t in taken]

        @pl.loop(0, rows // step)
        def _(i):
            at = pl.ds(pl.multiple_of(i * step, step), step)
            for (first, n, modules, has_extra), out in zip(plan, refs[n_in:]):
                values = [refs[first + k][0, at, :].astype(F32) for k in range(n)]
                for o, m in enumerate(modules):
                    acc = values[0] * gate[0][m]
                    for k in range(1, n):
                        acc += values[k] * gate[k][m]
                    if has_extra:
                        acc += refs[first + n][o, at, :].astype(F32)
                    out[o, at, :] = acc.astype(out.dtype)

    specs += [HBM] * len(earlier)
    return call(kernel, info, (ROWS // rows,), specs, out_specs, outs, (*operands, *earlier), 0)


def base_of(info, masters, moments, earlier=()):
    mods, own, width = masters[0].shape
    decay = 1.0 + momentum_decay
    a = 1.0 - outer_rate * decay
    b = -outer_rate * momentum_decay * momentum_decay

    def kernel(info_ref, m1, m2, v1, v2, *refs):
        for level, (m, v) in enumerate(((m1, v1), (m2, v2))):
            refs[-1][0, level * mods : (level + 1) * mods] = (a * m[...] + b * v[...]).astype(BF)

    spec = pl.BlockSpec((mods, own, COLS), lambda j, s: (0, 0, j))
    return call(
        kernel,
        info,
        (width // COLS,),
        [spec] * 4 + [HBM] * len(earlier),
        pl.BlockSpec((1, 2 * mods, own, COLS), lambda j, s: (j, 0, 0, 0)),
        jax.ShapeDtypeStruct((width // COLS, 2 * mods, own, COLS), BF),
        (*masters, *moments, *earlier),
        6 * masters[0].size,
    )


def renew(factor, base, first, keep, halves, wholes, split, earlier=()):
    groups, _, own, cols = base.shape
    mods = keep.shape[0]
    n_half = [len(h) for h in halves]

    def kernel(factor_ref, ins, outs):
        base_ref, keep_ref, *refs = ins
        low, high = refs[: n_half[0]], refs[n_half[0] : sum(n_half)]
        rest = refs[sum(n_half) :]

        @pl.loop(0, groups)
        def _(s):
            at = pl.ds(pl.multiple_of(s * own, own), own)
            for m in range(mods):
                acc = keep_ref[m, at, :]
                for h in (low, high)[m // 2]:
                    acc += h[m % 2, at, :].astype(F32)
                for h in rest:
                    acc += h[m, at, :].astype(F32)
                value = (base_ref[s, first + m].astype(F32) + factor_ref[m] * acc).astype(BF)
                if split:
                    outs[m // 2][m % 2, at, :] = value
                else:
                    outs[0][m, at, :] = value

    outs = [block(mods // 2)] * 2 if split else [block(mods)]
    operands = (base, keep, *halves[0], *halves[1], *wholes)
    return whole(kernel, factor, operands, outs, 4 * keep.size, earlier)


def choose(info, level, steps, sources):
    rows = ROWS // 2
    operands, specs = [], []

    def spec(index):
        return pl.BlockSpec((1, rows, COLS), lambda i, s: (index(s), i, 0))

    for step in steps:
        for source in sources:
            operands += source
            if len(source) == 1:
                specs.append(spec(lambda s, t=step: module_of(s, level, t)))
            else:
                specs.append(spec(lambda s, t=step: jnp.minimum(module_of(s, level, t), 1)))
                specs.append(spec(lambda s, t=step: jnp.maximum(module_of(s, level, t) - 2, 0)))
    n = len(sources)

    def kernel(info_ref, *refs):
        at = 0
        for j, step in enumerate(steps):
            low = module_of(info_ref, level, step) < 2
            out = refs[len(operands) + j]
            for k, source in enumerate(sources):
                if len(source) == 1:
                    out[k] = refs[at][0]
                else:
                    @pl.when(low)
                    def _(at=at, k=k, out=out):
                        out[k] = refs[at][0]

                    @pl.when(jnp.logical_not(low))
                    def _(at=at, k=k, out=out):
                        out[k] = refs[at + 1][0]
                at += len(source)

    return call(
        kernel,
        info,
        (ROWS // rows,),
        specs,
        [pl.BlockSpec((n, rows, COLS), lambda i, s: (0, i, 0))] * len(steps),
        [block(n)] * len(steps),
        operands,
        0,
    )


def place(info, befores, jobs, earlier=()):
    n_in, n = len(jobs), sum(len(steps) for _, steps, _ in jobs)
    results = 1 + max(r for _, _, r in jobs)
    rest = list(befores) + list(earlier)

    def kernel(info_ref, *refs):
        sems = refs[-1]
        outs = refs[-1 - results : -1]
        copies = []
        for j, (_, steps, r) in enumerate(jobs):
            for k, step in enumerate(steps):
                start = pl.multiple_of(block_of(info_ref[0], *step) * ROWS, ROWS)
                target = outs[r].at[pl.ds(start, ROWS)]
                copies.append(pltpu.make_async_copy(refs[j].at[k], target, sems.at[len(copies)]))
        for copy in copies:
            copy.start()
        for copy in copies:
            copy.wait()

    return pl.pallas_call(
        kernel,
        out_shape=[jax.ShapeDtypeStruct((16 * ROWS, COLS), BF)] * results,
        in_specs=[SMEM] + [VMEM] * n_in + [HBM] * len(rest),
        out_specs=[HBM] * results,
        scratch_shapes=[pltpu.SemaphoreType.DMA((n,))],
        input_output_aliases={1 + n_in + k: k for k in range(len(befores))},
        compiler_params=pltpu.CompilerParams(vmem_limit_bytes=24 << 20),
        cost_estimate=pl.CostEstimate(flops=1, bytes_accessed=1, transcendentals=0),
    )(info, *[a for a, _, _ in jobs], *rest)


def body(
    activations,
    cotangent,
    first_weight,
    second_weight,
    first_master,
    second_master,
    first_moment,
    second_moment,
    routing,
):
    weight_in = first_weight[0]
    weight_out = second_weight[0]
    scale = weight_in.shape[0] ** (-0.5)
    info = jnp.concatenate([lax.axis_index("path")[None].astype(jnp.int32), routing.reshape(-1)])

    def factor_of(level):
        taken = jnp.sum((routing[:, level][:, None] == jnp.arange(4)[None, :]).astype(F32), axis=0)
        return (outer_rate * (1.0 + momentum_decay)) / taken

    factor1, factor2 = factor_of(0), factor_of(1)

    masters, moments = (first_master, second_master), (first_moment, second_moment)
    acts, cots = gather_rows(info, activations[0], cotangent[0])

    pres = [jnp.dot(a, weight_in, preferred_element_type=F32) * scale for a in acts]
    sigmas = [jax.nn.sigmoid(p) for p in pres]
    hiddens = [(p * s).astype(BF) for p, s in zip(pres, sigmas)]
    grads = []
    for c, p, s in zip(cots, pres, sigmas):
        grad_hidden = jnp.dot(c, weight_out, preferred_element_type=F32) * scale
        grads.append((grad_hidden * s * (1.0 + p * (1.0 - s))).astype(BF))

    def first_rows(kinds, *earlier):
        groups = [[(dxh, dy, dc) for dy in range(4)] for dxh, dc in kinds]
        return trained(info, acts, grads, weight_in, groups, scale, earlier)

    (to_core,) = first_rows([(0, 1)])
    from_core = over_path(to_core, 0, 0, 1)

    here2, up2, far2, down2 = trained(
        info, cots, hiddens, weight_out,
        [[(dxh, dy, dc) for dc in range(2) for dxh in range(2)] for dy in range(4)], scale,
        (to_core,),
    )
    got2 = [here2, over_path(far2, 0, 2, 0), over_path(up2, 0, 1, 0), over_path(down2, 0, 3, 0)]
    to_side, to_cross, here1 = first_rows([(1, 0), (1, 1), (0, 0)], from_core, here2)
    pieces1 = [over_path(to_side, 1, 0, 0), over_path(to_cross, 1, 0, 1), from_core, here1]

    base = base_of(info, masters, moments, (here1,))

    all4 = (0, 1, 2, 3)
    steps1 = [(1, 0, 0), (1, 0, 1), (0, 0, 1), (0, 0, 0)]

    def at(dy):
        return [(p, dy) for p in pieces1]

    def sums(*jobs, earlier=()):
        return combine(info, 0, steps1, jobs, earlier)

    far_low, far_high, up_high, down_low = sums(
        (at(2), (0, 1), None, BF),
        (at(2), (2, 3), None, BF),
        (at(1), (2, 3), None, BF),
        (at(3), (0, 1), None, BF),
        earlier=(base,),
    )
    part_low = over_path(far_low, 0, 1, 0)
    part_high = over_path(far_high, 0, 3, 0)
    up_high = over_path(up_high, 0, 1, 0)
    down_low = over_path(down_low, 0, 3, 0)

    mine2, for_core2 = join(info, got2, (far_low,))
    base = lax.all_to_all(base, "mod", 0, 0, tiled=True)
    swapped2 = over_path(for_core2, 0, 0, 1)
    steps2 = [(0, dy, dc) for dc in (0, 1) for dy in (0, 2, 3, 1)]

    def pieces2(dxh):
        return [(x, 2 * k + dxh) for x in (mine2, swapped2) for k in range(4)]

    (send2,) = combine(info, 1, steps2, [(pieces2(1), all4, None, BF)])
    arrived2 = over_path(send2, 1, 0, 0)

    up_low, down_high = sums(
        (at(1), (0, 1), part_low, BF), (at(3), (2, 3), part_high, BF), earlier=(send2,)
    )
    up_low = over_path(up_low, 0, 1, 0)
    down_high = over_path(down_high, 0, 3, 0)
    (keep1,) = sums((at(0), all4, None, F32))
    (keep2,) = combine(info, 1, steps2, [(pieces2(0), all4, None, F32)], (keep1,))

    low, high = renew(factor1, base, 0, keep1, ((up_low, down_low), (up_high, down_high)), (), True)
    below = (over_path(low, 0, 1, 0), over_path(high, 0, 1, 0))
    above = (over_path(low, 0, 3, 0), over_path(high, 0, 3, 0))
    far = (over_path(below[0], 0, 1, 0), over_path(above[1], 0, 3, 0))
    rings = [(low, high), above, far, below]

    (new2,) = renew(factor2, base, 4, keep2, ((), ()), (arrived2,), False, (low,))
    side2 = over_path(new2, 1, 0, 0)
    kinds = [(0, 0), (1, 0), (0, 1), (1, 1)]
    around2 = [(new2,), (side2,), (over_path(new2, 0, 0, 1),), (over_path(side2, 0, 0, 1),)]

    def rows1(dxh, dc):
        return [(dxh, dy, dc) for dy in range(4)]

    def rows2(dy):
        return [(dxh, dy, dc) for dxh, dc in kinds]

    to_far, to_up, to_down = choose(info, 1, [(0, dy, 0) for dy in (2, 1, 3)], around2)
    came2 = {2: over_path(to_far, 0, 2, 0), 3: over_path(to_up, 0, 1, 0), 1: over_path(to_down, 0, 3, 0)}
    (here2,) = choose(info, 1, [(0, 0, 0)], around2)
    to_side, to_cross = choose(info, 0, [(1, 0, 0), (1, 0, 1)], rings)
    to_core, here1 = choose(info, 0, [(0, 0, 1), (0, 0, 0)], rings)
    came1 = {
        (1, 0): over_path(to_side, 1, 0, 0),
        (1, 1): over_path(to_cross, 1, 0, 1),
        (0, 1): over_path(to_core, 0, 0, 1),
    }

    results = place(
        info,
        (),
        [(here1, rows1(0, 0), 0), (came1[0, 1], rows1(0, 1), 0), (here2, rows2(0), 1)],
    )
    results = place(
        info,
        results,
        [(came1[1, 0], rows1(1, 0), 0), (came1[1, 1], rows1(1, 1), 0)]
        + [(came2[dy], rows2(dy), 1) for dy in (2, 3, 1)],
    )
    return (results[0][None], results[1][None])


def solution(mesh):
    return jax.shard_map(
        body,
        mesh=mesh,
        in_specs=(
            P("path", "mod", None),
            P("path", "mod", None),
            P("path", None, "mod"),
            P("path", None, "mod"),
            P(None, ("path", "mod"), None),
            P(None, ("path", "mod"), None),
            P(None, ("path", "mod"), None),
            P(None, ("path", "mod"), None),
            P(),
        ),
        out_specs=(P("path", None, "mod"), P("path", None, "mod")),
        check_vma=False,
    )
```

```python
import functools

import jax
import jax.numpy as jnp
from jax import lax
from jax.experimental import pallas as pl
from jax.experimental.pallas import tpu as pltpu
from jax.sharding import PartitionSpec as P

inner_rate = 1.0
outer_rate = 0.7
momentum_decay = 0.9

ROWS = 256
COLS = 512
HBM = pl.BlockSpec(memory_space=pl.ANY)
VMEM = pl.BlockSpec(memory_space=pltpu.VMEM)
SMEM = pl.BlockSpec(memory_space=pltpu.SMEM)
BF = jnp.bfloat16
F32 = jnp.float32


def path_pairs(dxh, dy, dc):
    return [
        ((xh * 4 + y) * 2 + c, ((xh ^ dxh) * 4 + (y + dy) % 4) * 2 + (c ^ dc))
        for xh in range(2)
        for y in range(4)
        for c in range(2)
    ]


def mod_pairs(dxl, dz):
    return [(xl * 4 + z, (xl ^ dxl) * 4 + (z + dz) % 4) for xl in range(2) for z in range(4)]


def over_path(x, dxh, dy, dc):
    return lax.ppermute(x, "path", path_pairs(dxh, dy, dc))


def over_mod(x, dxl, dz):
    return lax.ppermute(x, "mod", mod_pairs(dxl, dz))


def block_of(me, dxh, dy, dc):
    xh, y, c = me // 8, (me // 2) % 4, me % 2
    return (((xh + dxh) % 2) * 4 + (y + dy) % 4) * 2 + (c + dc) % 2


def module_of(info, level, step):
    return info[1 + 2 * block_of(info[0], *step) + level]


def call(kernel, info, grid, in_specs, out_specs, outs, operands, flops, aliases=None):
    moved = sum(x.size * x.dtype.itemsize for x in operands)
    return pl.pallas_call(
        kernel,
        out_shape=outs,
        grid_spec=pltpu.PrefetchScalarGridSpec(
            num_scalar_prefetch=1, grid=grid, in_specs=in_specs, out_specs=out_specs
        ),
        input_output_aliases=aliases or {},
        compiler_params=pltpu.CompilerParams(vmem_limit_bytes=24 << 20),
        cost_estimate=pl.CostEstimate(flops=1, bytes_accessed=1, transcendentals=0),
    )(info, *operands)


def whole(kernel, info, operands, outs, flops, earlier=()):
    n_in, n_wait = len(operands), len(earlier)

    def run(info_ref, *refs):
        kernel(info_ref, refs[:n_in], refs[n_in + n_wait :])

    moved = sum(x.size * x.dtype.itemsize for x in operands)
    return pl.pallas_call(
        run,
        out_shape=outs,
        in_specs=[SMEM] + [VMEM] * (n_in + n_wait),
        out_specs=[VMEM] * len(outs),
        compiler_params=pltpu.CompilerParams(vmem_limit_bytes=8 << 20),
        cost_estimate=pl.CostEstimate(flops=1, bytes_accessed=1, transcendentals=0),
    )(info, *operands, *earlier)


def block(*lead, dtype=BF):
    return jax.ShapeDtypeStruct((*lead, ROWS, COLS), dtype)


def lay(info, arrays, earlier=()):
    flat = [x for a in arrays for x in (a if isinstance(a, tuple) else (a,))]
    kinds = [isinstance(a, tuple) for a in arrays]
    rows, width = (arrays[0][0].shape if kinds[0] else arrays[0].shape[1:])

    def kernel(info_ref, ins, outs):
        at = 0
        for k, pair in enumerate(kinds):
            for j in range(2):
                x = ins[at + j][...] if pair else ins[at][j]
                outs[j][k * rows : (k + 1) * rows, :] = x
            at += 2 if pair else 1

    out = jax.ShapeDtypeStruct((rows * len(arrays), width), BF)
    return whole(kernel, info, flat, [out, out], 0, earlier)


def gather_rows(info, a, c):
    def stack(a_ref, c_ref, out, sems):
        copies = [
            pltpu.make_async_copy(x, out.at[k], sems.at[k]) for k, x in enumerate((a_ref, c_ref))
        ]
        for copy in copies:
            copy.start()
        for copy in copies:
            copy.wait()

    both = pl.pallas_call(
        stack,
        out_shape=jax.ShapeDtypeStruct((2, *a.shape), BF),
        in_specs=[pl.BlockSpec(memory_space=pltpu.HBM)] * 2,
        out_specs=VMEM,
        scratch_shapes=[pltpu.SemaphoreType.DMA((2,))],
        cost_estimate=pl.CostEstimate(flops=1, bytes_accessed=1, transcendentals=0),
    )(a, c)
    below, above, side = over_mod(both, 0, 1), over_mod(both, 0, 3), over_mod(both, 1, 0)
    far = (over_mod(below[0], 0, 1), over_mod(above[1], 0, 3))
    side_below, side_above = over_mod(side, 0, 1), over_mod(side, 0, 3)
    side_far = tuple(over_mod(x, 1, 0) for x in far)
    first = lay(info, [both, below, above, side], far)
    second = lay(info, [far, side_below, side_above, side_far])
    return tuple(zip(first, second))


def trained(info, rows, grads, weight, groups, scale, earlier=()):
    def kernel(info_ref, ins, outs):
        a0, a1, g0, g1, w = ins
        dims = (((0,), (0,)), ((), ()))
        for out, steps in zip(outs, groups):
            for k, step in enumerate(steps):
                start = pl.multiple_of(block_of(info_ref[0], *step) * ROWS, ROWS)
                at = pl.ds(start, ROWS)
                grad = lax.dot_general(a0[:, at], g0[...], dims, preferred_element_type=F32)
                grad += lax.dot_general(a1[:, at], g1[...], dims, preferred_element_type=F32)
                out[k] = (w[at, :].astype(F32) - (inner_rate * scale) * grad).astype(BF)

    n = sum(len(g) for g in groups)
    return whole(
        kernel,
        info,
        (*rows, *grads, weight),
        [block(len(g)) for g in groups],
        n * 4 * ROWS * COLS * rows[0].shape[0],
        earlier,
    )


def join(info, arrays, earlier=()):
    n, rows = arrays[0].shape[0] // 2, ROWS // 2

    def kernel(info_ref, *refs):
        for k in range(len(arrays)):
            refs[-2][k * n : (k + 1) * n] = refs[k][:n]
            refs[-1][k * n : (k + 1) * n] = refs[k][n:]

    out = pl.BlockSpec((n * len(arrays), rows, COLS), lambda i, s: (0, i, 0))
    return call(
        kernel,
        info,
        (ROWS // rows,),
        [pl.BlockSpec((2 * n, rows, COLS), lambda i, s: (0, i, 0))] * len(arrays) + [HBM] * len(earlier),
        [out, out],
        [block(n * len(arrays))] * 2,
        (*arrays, *earlier),
        0,
    )


def combine(info, level, steps, jobs, earlier=()):
    rows, step = ROWS // 2, 16
    operands, specs, outs, out_specs, plan = [], [], [], [], []
    for pieces, modules, extra, dtype in jobs:
        first = len(operands)
        for array, at in pieces:
            operands.append(array)
            specs.append(pl.BlockSpec((1, rows, COLS), functools.partial(lambda b, i, s: (b, i, 0), at)))
        both = pl.BlockSpec((len(modules), rows, COLS), lambda i, s: (0, i, 0))
        if extra is not None:
            operands.append(extra)
            specs.append(both)
        plan.append((first, len(pieces), modules, extra is not None))
        outs.append(block(len(modules), dtype=dtype))
        out_specs.append(both)
    n_in = len(operands) + len(earlier)

    def kernel(info_ref, *refs):
        taken = [module_of(info_ref, level, s) for s in steps]
        gate = [[jnp.where(t == m, 1.0, 0.0) for m in range(4)] for t in taken]

        @pl.loop(0, rows // step)
        def _(i):
            at = pl.ds(pl.multiple_of(i * step, step), step)
            for (first, n, modules, has_extra), out in zip(plan, refs[n_in:]):
                values = [refs[first + k][0, at, :].astype(F32) for k in range(n)]
                for o, m in enumerate(modules):
                    acc = values[0] * gate[0][m]
                    for k in range(1, n):
                        acc += values[k] * gate[k][m]
                    if has_extra:
                        acc += refs[first + n][o, at, :].astype(F32)
                    out[o, at, :] = acc.astype(out.dtype)

    specs += [HBM] * len(earlier)
    return call(kernel, info, (ROWS // rows,), specs, out_specs, outs, (*operands, *earlier), 0)


def base_of(info, masters, moments, earlier=()):
    mods, own, width = masters[0].shape
    decay = 1.0 + momentum_decay
    a = 1.0 - outer_rate * decay
    b = -outer_rate * momentum_decay * momentum_decay

    def kernel(info_ref, m1, m2, v1, v2, *refs):
        for level, (m, v) in enumerate(((m1, v1), (m2, v2))):
            refs[-1][0, level * mods : (level + 1) * mods] = (a * m[...] + b * v[...]).astype(BF)

    spec = pl.BlockSpec((mods, own, COLS), lambda j, s: (0, 0, j))
    return call(
        kernel,
        info,
        (width // COLS,),
        [spec] * 4 + [HBM] * len(earlier),
        pl.BlockSpec((1, 2 * mods, own, COLS), lambda j, s: (j, 0, 0, 0)),
        jax.ShapeDtypeStruct((width // COLS, 2 * mods, own, COLS), BF),
        (*masters, *moments, *earlier),
        6 * masters[0].size,
    )


def renew(factor, base, first, keep, halves, wholes, split, earlier=()):
    groups, _, own, cols = base.shape
    mods = keep.shape[0]
    n_half = [len(h) for h in halves]

    def kernel(factor_ref, ins, outs):
        base_ref, keep_ref, *refs = ins
        low, high = refs[: n_half[0]], refs[n_half[0] : sum(n_half)]
        rest = refs[sum(n_half) :]

        @pl.loop(0, groups)
        def _(s):
            at = pl.ds(pl.multiple_of(s * own, own), own)
            for m in range(mods):
                acc = keep_ref[m, at, :]
                for h in (low, high)[m // 2]:
                    acc += h[m % 2, at, :].astype(F32)
                for h in rest:
                    acc += h[m, at, :].astype(F32)
                value = (base_ref[s, first + m].astype(F32) + factor_ref[m] * acc).astype(BF)
                if split:
                    outs[m // 2][m % 2, at, :] = value
                else:
                    outs[0][m, at, :] = value

    outs = [block(mods // 2)] * 2 if split else [block(mods)]
    operands = (base, keep, *halves[0], *halves[1], *wholes)
    return whole(kernel, factor, operands, outs, 4 * keep.size, earlier)


def choose(info, level, steps, sources):
    rows = ROWS // 2
    operands, specs = [], []

    def spec(index):
        return pl.BlockSpec((1, rows, COLS), lambda i, s: (index(s), i, 0))

    for step in steps:
        for source in sources:
            operands += source
            if len(source) == 1:
                specs.append(spec(lambda s, t=step: module_of(s, level, t)))
            else:
                specs.append(spec(lambda s, t=step: jnp.minimum(module_of(s, level, t), 1)))
                specs.append(spec(lambda s, t=step: jnp.maximum(module_of(s, level, t) - 2, 0)))
    n = len(sources)

    def kernel(info_ref, *refs):
        at = 0
        for j, step in enumerate(steps):
            low = module_of(info_ref, level, step) < 2
            out = refs[len(operands) + j]
            for k, source in enumerate(sources):
                if len(source) == 1:
                    out[k] = refs[at][0]
                else:
                    @pl.when(low)
                    def _(at=at, k=k, out=out):
                        out[k] = refs[at][0]

                    @pl.when(jnp.logical_not(low))
                    def _(at=at, k=k, out=out):
                        out[k] = refs[at + 1][0]
                at += len(source)

    return call(
        kernel,
        info,
        (ROWS // rows,),
        specs,
        [pl.BlockSpec((n, rows, COLS), lambda i, s: (0, i, 0))] * len(steps),
        [block(n)] * len(steps),
        operands,
        0,
    )


def place(info, befores, jobs, earlier=()):
    n_in, n = len(jobs), sum(len(steps) for _, steps, _ in jobs)
    results = 1 + max(r for _, _, r in jobs)
    rest = list(befores) + list(earlier)

    def kernel(info_ref, *refs):
        sems = refs[-1]
        outs = refs[-1 - results : -1]
        copies = []
        for j, (_, steps, r) in enumerate(jobs):
            for k, step in enumerate(steps):
                start = pl.multiple_of(block_of(info_ref[0], *step) * ROWS, ROWS)
                target = outs[r].at[pl.ds(start, ROWS)]
                copies.append(pltpu.make_async_copy(refs[j].at[k], target, sems.at[len(copies)]))
        for copy in copies:
            copy.start()
        for copy in copies:
            copy.wait()

    return pl.pallas_call(
        kernel,
        out_shape=[jax.ShapeDtypeStruct((16 * ROWS, COLS), BF)] * results,
        in_specs=[SMEM] + [VMEM] * n_in + [HBM] * len(rest),
        out_specs=[HBM] * results,
        scratch_shapes=[pltpu.SemaphoreType.DMA((n,))],
        input_output_aliases={1 + n_in + k: k for k in range(len(befores))},
        compiler_params=pltpu.CompilerParams(vmem_limit_bytes=24 << 20),
        cost_estimate=pl.CostEstimate(flops=1, bytes_accessed=1, transcendentals=0),
    )(info, *[a for a, _, _ in jobs], *rest)


def body(
    activations,
    cotangent,
    first_weight,
    second_weight,
    first_master,
    second_master,
    first_moment,
    second_moment,
    routing,
):
    weight_in = first_weight[0]
    weight_out = second_weight[0]
    scale = weight_in.shape[0] ** (-0.5)
    info = jnp.concatenate([lax.axis_index("path")[None].astype(jnp.int32), routing.reshape(-1)])

    def factor_of(level):
        taken = jnp.sum((routing[:, level][:, None] == jnp.arange(4)[None, :]).astype(F32), axis=0)
        return (outer_rate * (1.0 + momentum_decay)) / taken

    factor1, factor2 = factor_of(0), factor_of(1)

    masters, moments = (first_master, second_master), (first_moment, second_moment)
    acts, cots = gather_rows(info, activations[0], cotangent[0])

    pres = [jnp.dot(a, weight_in, preferred_element_type=F32) * scale for a in acts]
    sigmas = [jax.nn.sigmoid(p) for p in pres]
    hiddens = [(p * s).astype(BF) for p, s in zip(pres, sigmas)]
    grads = []
    for c, p, s in zip(cots, pres, sigmas):
        grad_hidden = jnp.dot(c, weight_out, preferred_element_type=F32) * scale
        grads.append((grad_hidden * s * (1.0 + p * (1.0 - s))).astype(BF))

    def first_rows(kinds, *earlier):
        groups = [[(dxh, dy, dc) for dy in range(4)] for dxh, dc in kinds]
        return trained(info, acts, grads, weight_in, groups, scale, earlier)

    (to_core,) = first_rows([(0, 1)])
    from_core = over_path(to_core, 0, 0, 1)
    to_side, to_cross, here1 = first_rows([(1, 0), (1, 1), (0, 0)], to_core)
    pieces1 = [over_path(to_side, 1, 0, 0), over_path(to_cross, 1, 0, 1), from_core, here1]

    here2, up2, far2, down2 = trained(
        info, cots, hiddens, weight_out,
        [[(dxh, dy, dc) for dc in range(2) for dxh in range(2)] for dy in range(4)], scale,
        (from_core, here1),
    )
    got2 = [here2, over_path(far2, 0, 2, 0), over_path(up2, 0, 1, 0), over_path(down2, 0, 3, 0)]

    base = base_of(info, masters, moments, (here2,))

    all4 = (0, 1, 2, 3)
    steps1 = [(1, 0, 0), (1, 0, 1), (0, 0, 1), (0, 0, 0)]

    def at(dy):
        return [(p, dy) for p in pieces1]

    def sums(*jobs, earlier=()):
        return combine(info, 0, steps1, jobs, earlier)

    far_low, far_high, up_high, down_low = sums(
        (at(2), (0, 1), None, BF),
        (at(2), (2, 3), None, BF),
        (at(1), (2, 3), None, BF),
        (at(3), (0, 1), None, BF),
        earlier=(base,),
    )
    part_low = over_path(far_low, 0, 1, 0)
    part_high = over_path(far_high, 0, 3, 0)
    up_high = over_path(up_high, 0, 1, 0)
    down_low = over_path(down_low, 0, 3, 0)

    mine2, for_core2 = join(info, got2, (far_low,))
    base = lax.all_to_all(base, "mod", 0, 0, tiled=True)
    swapped2 = over_path(for_core2, 0, 0, 1)
    steps2 = [(0, dy, dc) for dc in (0, 1) for dy in (0, 2, 3, 1)]

    def pieces2(dxh):
        return [(x, 2 * k + dxh) for x in (mine2, swapped2) for k in range(4)]

    (send2,) = combine(info, 1, steps2, [(pieces2(1), all4, None, BF)])
    arrived2 = over_path(send2, 1, 0, 0)

    up_low, down_high = sums(
        (at(1), (0, 1), part_low, BF), (at(3), (2, 3), part_high, BF), earlier=(send2,)
    )
    up_low = over_path(up_low, 0, 1, 0)
    down_high = over_path(down_high, 0, 3, 0)
    (keep1,) = sums((at(0), all4, None, F32))
    (keep2,) = combine(info, 1, steps2, [(pieces2(0), all4, None, F32)], (keep1,))

    low, high = renew(factor1, base, 0, keep1, ((up_low, down_low), (up_high, down_high)), (), True)
    below = (over_path(low, 0, 1, 0), over_path(high, 0, 1, 0))
    above = (over_path(low, 0, 3, 0), over_path(high, 0, 3, 0))
    far = (over_path(below[0], 0, 1, 0), over_path(above[1], 0, 3, 0))
    rings = [(low, high), above, far, below]

    (new2,) = renew(factor2, base, 4, keep2, ((), ()), (arrived2,), False, (low,))
    side2 = over_path(new2, 1, 0, 0)
    kinds = [(0, 0), (1, 0), (0, 1), (1, 1)]
    around2 = [(new2,), (side2,), (over_path(new2, 0, 0, 1),), (over_path(side2, 0, 0, 1),)]

    def rows1(dxh, dc):
        return [(dxh, dy, dc) for dy in range(4)]

    def rows2(dy):
        return [(dxh, dy, dc) for dxh, dc in kinds]

    to_far, to_up, to_down = choose(info, 1, [(0, dy, 0) for dy in (2, 1, 3)], around2)
    came2 = {2: over_path(to_far, 0, 2, 0), 3: over_path(to_up, 0, 1, 0), 1: over_path(to_down, 0, 3, 0)}
    (here2,) = choose(info, 1, [(0, 0, 0)], around2)
    to_side, to_cross = choose(info, 0, [(1, 0, 0), (1, 0, 1)], rings)
    to_core, here1 = choose(info, 0, [(0, 0, 1), (0, 0, 0)], rings)
    came1 = {
        (1, 0): over_path(to_side, 1, 0, 0),
        (1, 1): over_path(to_cross, 1, 0, 1),
        (0, 1): over_path(to_core, 0, 0, 1),
    }

    results = place(
        info,
        (),
        [(here1, rows1(0, 0), 0), (came1[0, 1], rows1(0, 1), 0), (here2, rows2(0), 1)],
    )
    results = place(
        info,
        results,
        [(came1[1, 0], rows1(1, 0), 0), (came1[1, 1], rows1(1, 1), 0)]
        + [(came2[dy], rows2(dy), 1) for dy in (2, 3, 1)],
    )
    return (results[0][None], results[1][None])


def solution(mesh):
    return jax.shard_map(
        body,
        mesh=mesh,
        in_specs=(
            P("path", "mod", None),
            P("path", "mod", None),
            P("path", None, "mod"),
            P("path", None, "mod"),
            P(None, ("path", "mod"), None),
            P(None, ("path", "mod"), None),
            P(None, ("path", "mod"), None),
            P(None, ("path", "mod"), None),
            P(),
        ),
        out_specs=(P("path", None, "mod"), P("path", None, "mod")),
        check_vma=False,
    )
```
